32 devices in a mesh: dp: 8 (over z, y), row: 2 (over core), col: 2 (over x).
Axes of the slice: x: 2, y: 2, z: 4, core: 2. Of those that a mesh axis runs over, the one named last changes fastest.
Arguments:
- tokens: bfloat16 [2, 8192, 1536], P('col', ('dp', 'row')), may hold values from -18 to 18
- cotangent: float32 [2, 8192, 1536], P('col', ('dp', 'row')), may hold values from -6 to 6
- routes: int32 [4, 16384], P(None, 'dp'), may hold values from 0 to 31, as said below
- route_gates: float32 [4, 16384], P(None, 'dp'), may hold values from 0.5 to 1.5
- block_ids: int32 [16, 1024], P(('dp', 'col')), may hold values from 0 to 7, never falling along the last dimension, each value on 1 to 256 neighbouring positions
- w_qkv: bfloat16 [1536, 2, 1024], P('col', 'row'), may hold values from -0.15625 to 0.15625
- w_out: bfloat16 [2, 768, 1536], P('row', None, 'col'), may hold values from -2 to 2
- w_gate_up: bfloat16 [32, 1536, 2, 768], P(None, 'col', None, 'row'), may hold values from -0.15625 to 0.15625
- w_down: bfloat16 [32, 768, 1536], P(None, 'row', 'col'), may hold values from -0.21875 to 0.21875
- gains: float32 [2, 1536], P(None, 'col'), may hold values from 0.5 to 1.5
- gain_first: float32 [2, 1536], P(None, 'col'), may hold values from -1536 to 1536
- gain_second: float32 [2, 1536], P(None, 'col'), may hold values from 65536 to 262144
- qkv_master: float32 [1536, 2, 1024], P(('col', 'dp'), 'row'), may hold values from -0.15625 to 0.15625
- qkv_first: float32 [1536, 2, 1024], P(('col', 'dp'), 'row'), may hold values from -1536 to 1536
- qkv_second: float32 [1536, 2, 1024], P(('col', 'dp'), 'row'), may hold values from 65536 to 262144
- out_master: float32 [2, 768, 1536], P('row', None, ('col', 'dp')), may hold values from -2 to 2
- out_first: float32 [2, 768, 1536], P('row', None, ('col', 'dp')), may hold values from -48 to 48
- out_second: float32 [2, 768, 1536], P('row', None, ('col', 'dp')), may hold values from 64 to 256
- gate_up_master: float32 [32, 1536, 2, 768], P('dp', 'col', None, 'row'), may hold values from -0.15625 to 0.15625
- gate_up_first: float32 [32, 1536, 2, 768], P('dp', 'col', None, 'row'), may hold values from -192 to 192
- gate_up_second: float32 [32, 1536, 2, 768], P('dp', 'col', None, 'row'), may hold values from 1024 to 4096
- down_master: float32 [32, 768, 1536], P('dp', 'row', 'col'), may hold values from -0.21875 to 0.21875
- down_first: float32 [32, 768, 1536], P('dp', 'row', 'col'), may hold values from -192 to 192
- down_second: float32 [32, 768, 1536], P('dp', 'row', 'col'), may hold values from 1024 to 4096
Outputs:
- block_output: float32 [2, 8192, 1536], P('col', ('dp', 'row'))
- input_grad: float32 [2, 8192, 1536], P('col', ('dp', 'row'))
- qkv_weight: float32 [1536, 2, 1024], P(('col', 'dp'), 'row')
- qkv_moment_one: float32 [1536, 2, 1024], P(('col', 'dp'), 'row')
- qkv_moment_two: float32 [1536, 2, 1024], P(('col', 'dp'), 'row')
- qkv_copy: bfloat16 [1536, 2, 1024], P(('col', 'dp'), 'row')
- out_weight: float32 [2, 768, 1536], P('row', None, ('col', 'dp'))
- out_moment_one: float32 [2, 768, 1536], P('row', None, ('col', 'dp'))
- out_moment_two: float32 [2, 768, 1536], P('row', None, ('col', 'dp'))
- out_copy: bfloat16 [2, 768, 1536], P('row', None, ('col', 'dp'))
- gate_up_weight: float32 [32, 1536, 2, 768], P('dp', 'col', None, 'row')
- gate_up_moment_one: float32 [32, 1536, 2, 768], P('dp', 'col', None, 'row')
- gate_up_moment_two: float32 [32, 1536, 2, 768], P('dp', 'col', None, 'row')
- gate_up_copy: bfloat16 [32, 1536, 2, 768], P('dp', 'col', None, 'row')
- down_weight: float32 [32, 768, 1536], P('dp', 'row', 'col')
- down_moment_one: float32 [32, 768, 1536], P('dp', 'row', 'col')
- down_moment_two: float32 [32, 768, 1536], P('dp', 'row', 'col')
- down_copy: bfloat16 [32, 768, 1536], P('dp', 'row', 'col')
- gains_new: float32 [2, 1536], P(None, 'col')
- gains_moment_one: float32 [2, 1536], P(None, 'col')
- gains_moment_two: float32 [2, 1536], P(None, 'col')
- clip_factors: float32 [12], replicated
The draws below stay inside these ranges and needn't reach their ends.
Inputs may be any that keep to these rules, and one draw needn't show every extreme that they name: `routes`: each token names 4 different experts; among the 2048 tokens of one index of dp no expert is named by more than 320 tokens, some expert by exactly 320, and every expert by at least one. `block_ids`: along each sequence the block numbers never fall, start at 0 and rise by one; a block has 1 to 256 positions.
All inputs are finite; a program needn't handle non-finite values.
Results may differ from the reference program's by a relative error of at most 0.014.
Values may be sent and summed in bfloat16 or wider, within the bound.
No kernel may reach another device: no remote copies, remote signals or barrier semaphores. Data moves between devices by JAX's collectives and lax.ppermute only.
A program may use at most 768 MiB of HBM per device.

```python
import math
from functools import partial
import jax
import jax.numpy as jnp
import numpy as np
from jax import lax

D = 1536
HEADS = 12
KVH = 2
HD = 128
E = 32
FFE = 768
TOP = 4
GROUP = 6
QKW = 1024
LEN = 1024
BLK = 256
NBLK = 8
STEP = 5
TOK_DP = 2048
TOKENS = 16384
PAIRS = 8192
DBLK = 768
SEQS = 16
CAP = 320
N_DP = 8
N_COL = 2


def draw_tokens(key, part):
    key = jax.random.fold_in(key, 11)
    feature = jnp.arange(D // DBLK, dtype=jnp.int32)[:, None] * DBLK + jnp.arange(2 * DBLK, dtype=jnp.int32)[None, :] % DBLK
    ramp = (feature.astype(jnp.float32) / (D - 1))[:, None, :]
    shape = (D // DBLK, PAIRS, 2 * DBLK)
    base = jnp.clip(jax.random.normal(key, shape, jnp.float32), -6.0, 6.0)
    return (base * jnp.exp(jnp.log(3.0) * ramp)).astype(jnp.bfloat16)


def draw_routes(key, part):
    key = jax.random.fold_in(key, 23)
    blocks = TOKENS // TOK_DP
    mean_load = TOK_DP * TOP // E
    key_spread, key_label, key_order = jax.random.split(key, 3)
    spread = jax.random.randint(key_spread, (blocks, E // 2), 0, CAP - mean_load + 1, dtype=jnp.int32)
    spread = spread.at[:, 0].set(CAP - mean_load)
    counts = jnp.stack([mean_load + spread, mean_load - spread], axis=-1).reshape(blocks, E)
    labels = jax.vmap(lambda k: jax.random.permutation(k, E))(jax.random.split(key_label, blocks)).astype(jnp.int32)
    run_ends = jnp.cumsum(counts, axis=1)
    pick_index = jnp.arange(TOK_DP * TOP, dtype=jnp.int32)
    position = jax.vmap(lambda ends: jnp.searchsorted(ends, pick_index, side='right'))(run_ends).astype(jnp.int32)
    chosen = jnp.take_along_axis(labels, position, axis=1).reshape(blocks, TOP, TOK_DP)
    token_order = jax.vmap(lambda k: jax.random.permutation(k, TOK_DP))(jax.random.split(key_order, blocks)).astype(jnp.int32)
    chosen = jnp.take_along_axis(chosen, token_order[:, None, :], axis=2)
    return chosen.transpose(1, 0, 2).reshape(TOP, TOKENS).astype(jnp.int32)


def shard_levels(rng, extent, cuts, smallest, high):
    def one(dim, parts):
        draws = jax.random.uniform(jax.random.fold_in(jax.random.fold_in(rng, 6), dim), (parts,), jnp.float32, smallest / len(cuts), high / len(cuts))
        return jnp.repeat(jnp.exp(draws), extent[dim] // parts).reshape((-1,) + (1,) * (len(extent) - dim - 1))

    loudness = one(*cuts[0])
    for cut in cuts[1:]:
        loudness = loudness * one(*cut)
    return loudness


def profile(number_of, total, bound, slope):
    weights = [(1 << 20) // math.isqrt(grade ** slope) + 1 for grade in range(2, number_of + 1)]
    spare, given = total - bound - (number_of - 1), [1] * (number_of - 1)
    while spare > 0:
        movable = [i for i in range(number_of - 1) if given[i] < bound]
        mass, remaining = sum([weights[i] for i in movable]), spare
        for i in movable:
            addition = min(bound - given[i], max(1, remaining * weights[i] // mass), spare)
            given[i] = given[i] + addition
            spare = spare - addition
    return np.array([bound] + given)


def ragged_sizes(key, number_of, total, most, skew):
    if number_of == 2:
        one = jax.random.randint(key, (), max(1, total - most), min(most, total - 1) + 1)
        return jnp.stack([one, total - one])
    tallies = jnp.asarray(profile(number_of, total, most, skew), jnp.int32)
    couples = (number_of - 1) // 2
    giver, receiver = tallies[1:1 + 2 * couples:2], tallies[2:2 + 2 * couples:2]
    slack = jnp.minimum(giver - 1, most - receiver)
    passed = jax.random.randint(jax.random.fold_in(key, 1), (couples,), 0, 1 << 20) % (slack + 1)
    tallies = tallies.at[1:1 + 2 * couples:2].set(giver - passed).at[2:2 + 2 * couples:2].set(receiver + passed)
    return tallies[jax.random.permutation(jax.random.fold_in(key, 2), number_of)]


def bell_draw(own_key, shape, width, most, shards=(), kind=jnp.bfloat16):
    values = jax.random.normal(own_key, shape, jnp.float32) * width
    if len(shards) > 0:
        values = shard_levels(own_key, shape, shards, -0.22, 0.18) * values
    return jnp.clip(values, min=-most, max=most).astype(kind)


def setup_inputs(seed: int = 0) -> dict:
    key_list = jax.random.split(jax.random.key(seed), 25)
    tokens = draw_tokens(jax.random.fold_in(key_list[24], 71), 0)
    cotangent = bell_draw(key_list[1], (N_COL, PAIRS, 2 * DBLK), 1.0, 6.0, ((0, 2), (1, 16)), jnp.float32)
    routes = draw_routes(jax.random.fold_in(key_list[24], 71), 0)
    route_gates = jnp.clip(0.5 + 1.0 * jax.random.uniform(key_list[3], (TOP, TOKENS), jnp.float32) ** shard_levels(key_list[3], (TOP, TOKENS), ((1, 8),), -0.2, 0.2), 0.5, 1.5)
    block_ids = jax.vmap(lambda own: jnp.searchsorted(jnp.cumsum(ragged_sizes(own, NBLK, LEN, BLK, 1)), jnp.arange(LEN), side="right"))(jax.random.split(key_list[4], SEQS)).reshape((SEQS, LEN)).astype(jnp.int32)
    w_qkv = bell_draw(key_list[5], (D, KVH, QKW), D ** -0.5, 0.15625, ((0, 2), (1, 2)))
    w_out = bell_draw(key_list[6], (KVH, GROUP * HD, D), (max(D // 192, 1)) ** -0.5, 2.0, ((0, 2), (2, 2)))
    w_gate_up = bell_draw(key_list[7], (E, D, 2, FFE), D ** -0.5, 0.15625, ((1, 2), (3, 2)))
    w_down = bell_draw(key_list[8], (E, FFE, D), FFE ** -0.5, 0.21875, ((1, 2), (2, 2)))
    gains = jnp.clip(1.0 + 0.1 * jax.random.normal(key_list[9], (2, D), jnp.float32), 0.5, 1.5)
    gain_first = bell_draw(key_list[10], (2, D), ((4 * TOKENS) ** 0.5), 1536.0, ((1, 2),), jnp.float32)
    gain_second = jnp.clip(jnp.exp(math.log(262144.0) - 1.3862944 * jax.random.uniform(key_list[11], (2, D), jnp.float32) ** shard_levels(key_list[11], (2, D), ((1, 2),), -0.2, 0.2)), 65536.0, 262144.0)
    qkv_master = bell_draw(key_list[12], (D, KVH, QKW), D ** -0.5, 0.15625, ((0, 16), (1, 2)), jnp.float32)
    qkv_first = bell_draw(key_list[13], (D, KVH, QKW), ((4 * TOKENS) ** 0.5), 1536.0, ((0, 16), (1, 2)), jnp.float32)
    qkv_second = jnp.clip(jnp.exp(math.log(262144.0) - 1.3862944 * jax.random.uniform(key_list[14], (D, KVH, QKW), jnp.float32) ** shard_levels(key_list[14], (D, KVH, QKW), ((0, 16), (1, 2)), -0.2, 0.2)), 65536.0, 262144.0)
    out_master = bell_draw(key_list[15], (KVH, GROUP * HD, D), (max(D // 192, 1)) ** -0.5, 2.0, ((0, 2), (2, 16)), jnp.float32)
    out_first = bell_draw(key_list[16], (KVH, GROUP * HD, D), ((TOKENS // 256) ** 0.5), 48.0, ((0, 2), (2, 16)), jnp.float32)
    out_second = jnp.clip(jnp.exp(math.log(256.0) - 1.3862944 * jax.random.uniform(key_list[17], (KVH, GROUP * HD, D), jnp.float32) ** shard_levels(key_list[17], (KVH, GROUP * HD, D), ((0, 2), (2, 16)), -0.2, 0.2)), 64.0, 256.0)
    gate_up_master = bell_draw(key_list[18], (E, D, 2, FFE), D ** -0.5, 0.15625, ((0, 8), (1, 2), (3, 2)), jnp.float32)
    gate_up_first = bell_draw(key_list[19], (E, D, 2, FFE), ((TOKENS // 16) ** 0.5), 192.0, ((0, 8), (1, 2), (3, 2)), jnp.float32)
    gate_up_second = jnp.clip(jnp.exp(math.log(4096.0) - 1.3862944 * jax.random.uniform(key_list[20], (E, D, 2, FFE), jnp.float32) ** shard_levels(key_list[20], (E, D, 2, FFE), ((0, 8), (1, 2), (3, 2)), -0.2, 0.2)), 1024.0, 4096.0)
    down_master = bell_draw(key_list[21], (E, FFE, D), FFE ** -0.5, 0.21875, ((0, 8), (1, 2), (2, 2)), jnp.float32)
    down_first = bell_draw(key_list[22], (E, FFE, D), ((TOKENS // 16) ** 0.5), 192.0, ((0, 8), (1, 2), (2, 2)), jnp.float32)
    down_second = jnp.clip(jnp.exp(math.log(4096.0) - 1.3862944 * jax.random.uniform(key_list[23], (E, FFE, D), jnp.float32) ** shard_levels(key_list[23], (E, FFE, D), ((0, 8), (1, 2), (2, 2)), -0.2, 0.2)), 1024.0, 4096.0)
    return {"tokens": tokens, "cotangent": cotangent, "routes": routes, "route_gates": route_gates, "block_ids": block_ids, "w_qkv": w_qkv, "w_out": w_out, "w_gate_up": w_gate_up, "w_down": w_down, "gains": gains, "gain_first": gain_first, "gain_second": gain_second, "qkv_master": qkv_master, "qkv_first": qkv_first, "qkv_second": qkv_second, "out_master": out_master, "out_first": out_first, "out_second": out_second, "gate_up_master": gate_up_master, "gate_up_first": gate_up_first, "gate_up_second": gate_up_second, "down_master": down_master, "down_first": down_first, "down_second": down_second}


EPS_NORM = 1e-06
BETA_ONE = 0.5
BETA_TWO = 0.5
ADAM_EPS = 1e-08
DECAY_RATE = 0.1
TAU_CLIP = 3.0
HIGHEST = lax.Precision.HIGHEST

@jax.custom_vjp
def low(v):
    return lax.optimization_barrier(v.astype(jnp.bfloat16)).astype(jnp.float32)

@jax.custom_vjp
def low_back(v):
    return v

def low_keep(v):
    return (low(v), None)

def low_pass(kept, grad):
    return (grad,)

def back_keep(v):
    return (v, None)

def back_low(kept, grad):
    return (low(grad),)
low.defvjp(low_keep, low_pass)
low_back.defvjp(back_keep, back_low)

def rounded_both(values):
    return low_back(low(values))

def unpack_rows(packed_rows):
    return packed_rows.reshape(N_COL, PAIRS, 2, DBLK).transpose(1, 2, 0, 3).reshape(TOKENS, D)

def pack_rows(values):
    return values.reshape(PAIRS, 2, N_COL, DBLK).transpose(2, 0, 1, 3).reshape(N_COL, PAIRS, 2 * DBLK)

def rms_norm(values, gain):
    factor = lax.rsqrt(lax.optimization_barrier(jnp.mean(values * values, axis=-1, keepdims=True)) + EPS_NORM)
    return values * factor * gain

def slot_table(routes, route_gates, experts, capacity):
    pairs = routes.reshape(-1).astype(jnp.int32)
    number = pairs.shape[0]
    order = jnp.argsort(pairs, stable=True).astype(jnp.int32)
    ranked = pairs[order]
    onehot = (pairs[:, None] == jnp.arange(experts, dtype=jnp.int32)[None, :]).astype(jnp.int32)
    totals = lax.optimization_barrier(jnp.sum(onehot, axis=0))
    starts = jnp.cumsum(totals) - totals
    place = ranked * capacity + jnp.arange(number, dtype=jnp.int32) - starts[ranked]
    owner = (order // routes.shape[1]).astype(jnp.int32)
    slot_tok = jnp.zeros((experts * capacity,), jnp.int32).at[place].set(owner)
    slot_gate = jnp.zeros((experts * capacity,), route_gates.dtype).at[place].set(route_gates.reshape(-1)[order])
    return (slot_tok, slot_gate)

def attend(packed, blocks):
    queries = packed[:, :, :GROUP, :]
    keys_in = packed[:, :, GROUP, :]
    values_in = packed[:, :, GROUP + 1, :]
    scores = jnp.einsum('qkgd,skd->kgqs', queries, keys_in, precision=HIGHEST) * HD ** (-0.5)
    scores = low_back(scores)
    allowed = blocks[None, :] <= blocks[:, None]
    masked = jnp.where(allowed[None, None], scores, -1e+30)
    row_top = lax.optimization_barrier(jnp.max(masked, axis=-1, keepdims=True))
    weights = jnp.exp(masked - row_top)
    probs_low = low(weights / lax.optimization_barrier(jnp.sum(weights, axis=-1, keepdims=True)))
    mixed = jnp.einsum('kgqs,skd->qkgd', probs_low, values_in, precision=HIGHEST)
    return (mixed.reshape(LEN, KVH * GROUP * HD), lax.optimization_barrier(jnp.max(row_top[..., 0], axis=-1)))

def expert_block(normed, slot_tok, slot_gate, w_gate_up, w_down):
    slot_rows = normed[slot_tok].reshape(E, CAP, D)
    gate_up = low_back(jnp.einsum('ecd,edgh->ecgh', slot_rows, w_gate_up, precision=HIGHEST))
    activity = jax.nn.silu(gate_up[:, :, 0]) * gate_up[:, :, 1]
    weighted = low(activity * slot_gate.reshape(E, CAP, 1))
    slot_out = jnp.einsum('ech,ehd->ecd', weighted, w_down, precision=HIGHEST).reshape(E * CAP, D)
    return jax.ops.segment_sum(slot_out, slot_tok, num_segments=TOK_DP)

def layer_forward(inputs, w_qkv, w_out, w_gate_up, w_down, gains, block_ids, slot_tok, slot_gate):
    normed_one = low(rms_norm(inputs, gains[0]))
    packed = rounded_both(jnp.dot(normed_one, w_qkv.reshape(D, KVH * QKW), precision=HIGHEST))
    packed = packed.reshape(SEQS, LEN, KVH, GROUP + 2, HD)
    attend_saved = jax.checkpoint(attend)
    mixed, tops = lax.map(lambda entries: attend_saved(entries[0], entries[1]), (packed, block_ids))
    heads = rounded_both(mixed.reshape(TOKENS, HEADS * HD))
    attn = low_back(jnp.dot(heads, w_out.reshape(HEADS * HD, D), precision=HIGHEST))
    hidden = inputs + attn
    normed_two = low(rms_norm(hidden, gains[1]))
    expert_saved = jax.checkpoint(expert_block)
    moe = lax.map(lambda entries: expert_saved(entries[0], entries[1], entries[2], w_gate_up, w_down), (normed_two.reshape(N_DP, TOK_DP, D), slot_tok, slot_gate))
    moe = low_back(moe.reshape(TOKENS, D))
    return (hidden + moe, lax.optimization_barrier(jnp.max(tops, axis=0)))

def adam_step(master, moment_one, moment_two, gradient, rate, decay):
    first = BETA_ONE * moment_one + (1.0 - BETA_ONE) * gradient
    second = BETA_TWO * moment_two + (1.0 - BETA_TWO) * gradient * gradient
    first_hat = first / (1.0 - BETA_ONE ** STEP)
    second_hat = second / (1.0 - BETA_TWO ** STEP)
    updated = master - rate * (first_hat / (jnp.sqrt(second_hat) + ADAM_EPS) + decay * master)
    return (updated, first, second)

def clip_scale(head_top):
    factors = TAU_CLIP / jnp.maximum(head_top, TAU_CLIP)
    query_scale = jnp.repeat(jnp.sqrt(factors), HD, axis=1)
    key_scale = jnp.repeat(jnp.sqrt(lax.optimization_barrier(jnp.min(factors, axis=1, keepdims=True))), HD, axis=1)
    return (factors, jnp.concatenate([query_scale, key_scale, jnp.ones_like(key_scale)], axis=1))

def reference(tokens, cotangent, routes, route_gates, block_ids, w_qkv, w_out, w_gate_up, w_down, gains, gain_first, gain_second, qkv_master, qkv_first, qkv_second, out_master, out_first, out_second, gate_up_master, gate_up_first, gate_up_second, down_master, down_first, down_second):
    table_fn = jax.vmap(partial(slot_table, experts=E, capacity=CAP))
    slot_tok, slot_gate = table_fn(routes.reshape(TOP, N_DP, TOK_DP).transpose(1, 2, 0), route_gates.reshape(TOP, N_DP, TOK_DP).transpose(1, 2, 0))

    def forward_fn(inputs, weights_qkv, weights_out, weights_gate_up, weights_down, gain_pair):
        return layer_forward(inputs, weights_qkv, weights_out, weights_gate_up, weights_down, gain_pair, block_ids, slot_tok, slot_gate)
    block_output, pullback, head_top = jax.vjp(forward_fn, unpack_rows(tokens.astype(jnp.float32)), w_qkv.astype(jnp.float32), w_out.astype(jnp.float32), w_gate_up.astype(jnp.float32), w_down.astype(jnp.float32), gains, has_aux=True)
    input_grad, grad_qkv, grad_out, grad_gate_up, grad_down, grad_gains = pullback(unpack_rows(cotangent))
    factors, column_scale = clip_scale(head_top)
    qkv_new, qkv_one, qkv_two = adam_step(qkv_master, qkv_first, qkv_second, grad_qkv, D ** (-0.5), DECAY_RATE)
    qkv_new = qkv_new * column_scale[None]
    out_new, out_one, out_two = adam_step(out_master, out_first, out_second, grad_out, max(D // 192, 1) ** (-0.5), DECAY_RATE)
    gate_up_new, gate_up_one, gate_up_two = adam_step(gate_up_master, gate_up_first, gate_up_second, grad_gate_up, D ** (-0.5), DECAY_RATE)
    down_new, down_one, down_two = adam_step(down_master, down_first, down_second, grad_down, FFE ** (-0.5), DECAY_RATE)
    gains_new, gains_one, gains_two = adam_step(gains, gain_first, gain_second, grad_gains, 0.2, 0.0)
    return (pack_rows(block_output), pack_rows(input_grad), qkv_new, qkv_one, qkv_two, qkv_new.astype(jnp.bfloat16), out_new, out_one, out_two, out_new.astype(jnp.bfloat16), gate_up_new, gate_up_one, gate_up_two, gate_up_new.astype(jnp.bfloat16), down_new, down_one, down_two, down_new.astype(jnp.bfloat16), gains_new, gains_one, gains_two, factors.reshape(HEADS))
```

```python
import functools

import jax
import jax.numpy as jnp
from jax import lax
from jax.experimental import pallas as pl
from jax.experimental.layout import Layout, with_layout_constraint
from jax.experimental.pallas import tpu as pltpu
from jax.sharding import PartitionSpec as P

D = 1536
KVH = 2
HD = 128
E = 32
FFE = 768
TOP = 4
GROUP = 6
LEN = 1024
STEP = 5


EPS_NORM = 1e-06
BETA_ONE = 0.5
BETA_TWO = 0.5
ADAM_EPS = 1e-08
DECAY_RATE = 0.1
TAU_CLIP = 3.0


QUERIES = 256
MIB = 1 << 20


def dot(left, right, left_dim=1, right_dim=0):
    return lax.dot_general(
        left, right, (((left_dim,), (right_dim,)), ((), ())), preferred_element_type=jnp.float32
    )


def pass_on(*refs):
    pass


def after(values, *earlier):
    return pl.pallas_call(
        pass_on,
        in_specs=[pl.BlockSpec(memory_space=pl.ANY)] * (1 + len(earlier)),
        out_specs=pl.BlockSpec(memory_space=pl.ANY),
        out_shape=jax.ShapeDtypeStruct(values.shape, values.dtype),
        input_output_aliases={0: 0},
        cost_estimate=pl.CostEstimate(flops=0, bytes_accessed=0, transcendentals=0),
    )(values, *earlier)


def col_total(values):
    return lax.psum(jnp.sum(values, axis=1), "col")


def butterfly(values, combine, axes):
    for axis in axes:
        count = lax.axis_size(axis)
        bit = 1
        while bit < count:
            pairs = [(i, i ^ bit) for i in range(count)]
            values = combine(values, lax.ppermute(values, axis, pairs))
            bit *= 2
    return values


def norm_backward(values, factor, gain, grad_normed):
    inner = col_total(values * gain[None, :] * grad_normed) / D
    grad_values = (
        factor[:, None] * gain[None, :] * grad_normed - values * (factor**3 * inner)[:, None]
    )
    grad_gain = jnp.sum(grad_normed * values * factor[:, None], axis=0)
    return (grad_values, grad_gain)


def to_owners(values, axes):
    return lax.all_to_all(values, axes, split_axis=0, concat_axis=0, tiled=True)


def slot_ranks(routes, route_gates):
    tokens = routes.shape[1]
    hits = routes[:, None, :] == jnp.arange(E, dtype=jnp.int32)[None, :, None]
    gates = jnp.sum(jnp.where(hits, route_gates[:, None, :], 0.0), axis=0)
    chosen = jnp.any(hits, axis=0)
    lanes = jnp.arange(128)
    upto = (lanes[:, None] <= lanes[None, :]).astype(jnp.bfloat16)
    runs = jnp.einsum(
        "ebt,ts->ebs",
        chosen.reshape(E, tokens // 128, 128).astype(jnp.bfloat16),
        upto,
        preferred_element_type=jnp.float32,
    ).astype(jnp.int32)
    totals = runs[:, :, -1]
    ranks = (runs + (jnp.cumsum(totals, axis=1) - totals)[:, :, None]).reshape(E, tokens) - 1
    return (jnp.where(chosen, ranks, -1), gates)


def key_reach(chunk):
    return min((chunk + 2) * QUERIES, LEN)


def scores_turned(queries, keys, id_row, id_col):
    scores = dot(keys, queries, 1, 1) * HD ** (-0.5)
    return jnp.where(id_col <= id_row, scores, -1e30)


def attend_kernel(query_ref, key_ref, value_ref, id_row_ref, id_col_ref, mixed_ref, log_ref, top_ref):
    value_turned = value_ref[...].T
    for chunk in range(LEN // QUERIES):
        rows = slice(chunk * QUERIES, (chunk + 1) * QUERIES)
        reach = key_reach(chunk)
        masked = scores_turned(
            query_ref[rows, :], key_ref[:reach, :], id_row_ref[:, rows], id_col_ref[:reach, :]
        )
        top = jnp.max(masked, axis=0, keepdims=True)
        weights = jnp.exp(masked - top)
        total = jnp.sum(weights, axis=0, keepdims=True)
        probs = (weights * (1.0 / total)).astype(jnp.bfloat16)
        mixed_ref[rows, :] = dot(value_turned[:, :reach], probs).T.astype(jnp.bfloat16)
        log_ref[0, :, rows] = top + jnp.log(total)
        top_ref[0, :, rows] = top


def attend_forward(packed, blocks):
    head = pl.BlockSpec((LEN, HD), lambda h: (0, h))
    row = pl.BlockSpec((1, 1, LEN), lambda h: (h, 0, 0))
    return pl.pallas_call(
        attend_kernel,
        grid=(GROUP,),
        in_specs=[
            head,
            pl.BlockSpec((LEN, HD), lambda h: (0, GROUP)),
            pl.BlockSpec((LEN, HD), lambda h: (0, GROUP + 1)),
            pl.BlockSpec((1, LEN), lambda h: (0, 0)),
            pl.BlockSpec((LEN, 1), lambda h: (0, 0)),
        ],
        out_specs=[head, row, row],
        out_shape=[
            jax.ShapeDtypeStruct((LEN, GROUP * HD), jnp.bfloat16),
            jax.ShapeDtypeStruct((GROUP, 1, LEN), jnp.float32),
            jax.ShapeDtypeStruct((GROUP, 1, LEN), jnp.float32),
        ],
        compiler_params=pltpu.CompilerParams(vmem_limit_bytes=40 * MIB),
        cost_estimate=pl.CostEstimate(
            flops=4 * GROUP * LEN * LEN * HD, bytes_accessed=4 * MIB, transcendentals=GROUP * LEN * LEN
        ),
    )(packed, packed, packed, blocks[None, :], blocks[:, None])


def attend_back_kernel(
    query_ref, key_ref, value_ref, grad_ref, log_ref, id_row_ref, id_col_ref, out_ref, keys_acc, values_acc
):
    head = pl.program_id(0)

    @pl.when(head == 0)
    def _():
        keys_acc[...] = jnp.zeros_like(keys_acc)
        values_acc[...] = jnp.zeros_like(values_acc)

    key_turned = key_ref[...].T
    for chunk in range(LEN // QUERIES):
        rows = slice(chunk * QUERIES, (chunk + 1) * QUERIES)
        reach = key_reach(chunk)
        queries = query_ref[rows, :]
        grads = grad_ref[rows, :]
        masked = scores_turned(queries, key_ref[:reach, :], id_row_ref[:, rows], id_col_ref[:reach, :])
        probs = jnp.exp(masked - log_ref[0, :, rows])
        grad_probs = dot(value_ref[:reach, :], grads, 1, 1)
        delta = jnp.sum(probs * grad_probs, axis=0, keepdims=True)
        grad_scores = (probs * (grad_probs - delta)).astype(jnp.bfloat16)
        values_acc[:reach, :] += dot(probs.astype(jnp.bfloat16), grads)
        keys_acc[:reach, :] += dot(grad_scores, queries)
        grad_query = dot(key_turned[:, :reach], grad_scores).T * HD ** (-0.5)
        lanes = pl.ds(pl.multiple_of(head * HD, HD), HD)
        out_ref[rows, lanes] = grad_query.astype(jnp.bfloat16)

    @pl.when(head == GROUP - 1)
    def _():
        out_ref[:, GROUP * HD : (GROUP + 1) * HD] = (keys_acc[...] * HD ** (-0.5)).astype(jnp.bfloat16)
        out_ref[:, (GROUP + 1) * HD :] = values_acc[...].astype(jnp.bfloat16)


def attend_backward(packed, blocks, log_total, grad_heads):
    head = pl.BlockSpec((LEN, HD), lambda h: (0, h))
    return pl.pallas_call(
        attend_back_kernel,
        grid=(GROUP,),
        in_specs=[
            head,
            pl.BlockSpec((LEN, HD), lambda h: (0, GROUP)),
            pl.BlockSpec((LEN, HD), lambda h: (0, GROUP + 1)),
            head,
            pl.BlockSpec((1, 1, LEN), lambda h: (h, 0, 0)),
            pl.BlockSpec((1, LEN), lambda h: (0, 0)),
            pl.BlockSpec((LEN, 1), lambda h: (0, 0)),
        ],
        out_specs=pl.BlockSpec((LEN, (GROUP + 2) * HD), lambda h: (0, 0)),
        out_shape=jax.ShapeDtypeStruct((LEN, (GROUP + 2) * HD), jnp.bfloat16),
        scratch_shapes=[pltpu.VMEM((LEN, HD), jnp.float32)] * 2,
        compiler_params=pltpu.CompilerParams(vmem_limit_bytes=40 * MIB),
        cost_estimate=pl.CostEstimate(
            flops=10 * GROUP * LEN * LEN * HD, bytes_accessed=6 * MIB, transcendentals=GROUP * LEN * LEN
        ),
    )(packed, packed, packed, grad_heads, log_total, blocks[None, :], blocks[:, None])


def expert_kernel(col_n, rows_ref, grads_ref, gate_ref, in_ref, down_ref, back_ref, weighted_ref, pair_ref):
    gate_up = dot(rows_ref[0, 0], in_ref[0])
    grad_weighted = dot(grads_ref[0, 0], down_ref[0], 1, 1)
    for c in range(1, col_n):
        gate_up += dot(rows_ref[0, c], in_ref[c])
        grad_weighted += dot(grads_ref[0, c], down_ref[c], 1, 1)
    gate_half, up_half, scale = gate_up[:, :FFE], gate_up[:, FFE:], gate_ref[0]
    sigmoid_gate = jax.nn.sigmoid(gate_half)
    silu_gate = gate_half * sigmoid_gate
    weighted_ref[0] = (silu_gate * up_half * scale).astype(jnp.bfloat16)
    grad_act = grad_weighted * scale
    grad_gate = grad_act * up_half * sigmoid_gate * (1.0 + gate_half * (1.0 - sigmoid_gate))
    pair_ref[0, :, :FFE] = grad_gate.astype(jnp.bfloat16)
    pair_ref[0, :, FFE:] = (grad_act * silu_gate).astype(jnp.bfloat16)
    for c in range(col_n):
        back_ref[0, c] = dot(pair_ref[0], in_ref[c], 1, 1).astype(jnp.bfloat16)


def expert_passes(slot_rows, slot_grads, gates, weights_in, weights_down):
    dl_n, col_n, slots, width = slot_rows.shape
    block = pl.BlockSpec((1, col_n, slots, width), lambda d: (d, 0, 0, 0))
    return pl.pallas_call(
        functools.partial(expert_kernel, col_n),
        grid=(dl_n,),
        in_specs=[
            block,
            block,
            pl.BlockSpec((1, slots, 1), lambda d: (d, 0, 0)),
            pl.BlockSpec(weights_in.shape, lambda d: (0, 0, 0)),
            pl.BlockSpec(weights_down.shape, lambda d: (0, 0, 0)),
        ],
        out_specs=[
            block,
            pl.BlockSpec((1, slots, FFE), lambda d: (d, 0, 0)),
            pl.BlockSpec((1, slots, 2 * FFE), lambda d: (d, 0, 0)),
        ],
        out_shape=[
            jax.ShapeDtypeStruct(slot_rows.shape, jnp.bfloat16),
            jax.ShapeDtypeStruct((dl_n, slots, FFE), jnp.bfloat16),
            jax.ShapeDtypeStruct((dl_n, slots, 2 * FFE), jnp.bfloat16),
        ],
        compiler_params=pltpu.CompilerParams(vmem_limit_bytes=56 * MIB),
        cost_estimate=pl.CostEstimate(
            flops=10 * dl_n * slots * D * FFE, bytes_accessed=30 * MIB, transcendentals=dl_n * slots * FFE
        ),
    )(slot_rows, slot_grads, gates, weights_in, weights_down)


def join_kernel(row_n, col_n, place_ref, *refs):
    count = row_n * col_n
    in_refs, down_refs, (in_out, down_out) = refs[:count], refs[count : 2 * count], refs[2 * count :]
    part = FFE // row_n
    for k in range(count):
        r = lax.rem(place_ref[0] + k // col_n, row_n)
        c = lax.rem(place_ref[1] + k % col_n, col_n)
        for g in range(2):
            lanes = pl.ds(pl.multiple_of(g * FFE + r * part, 128), part)
            in_out[c, :, lanes] = in_refs[k][g]
        down_out[c, pl.ds(pl.multiple_of(r * part, 128), part), :] = down_refs[k][...]


def join_weights(in_pieces, down_pieces, place, row_n, col_n):
    width = in_pieces[0].shape[1]
    return pl.pallas_call(
        functools.partial(join_kernel, row_n, col_n),
        in_specs=[pl.BlockSpec(memory_space=pltpu.SMEM)]
        + [pl.BlockSpec(memory_space=pltpu.VMEM)] * (2 * row_n * col_n),
        out_specs=[pl.BlockSpec(memory_space=pltpu.VMEM)] * 2,
        out_shape=[
            jax.ShapeDtypeStruct((col_n, width, 2 * FFE), jnp.bfloat16),
            jax.ShapeDtypeStruct((col_n, FFE, width), jnp.bfloat16),
        ],
        compiler_params=pltpu.CompilerParams(vmem_limit_bytes=40 * MIB),
        cost_estimate=pl.CostEstimate(flops=0, bytes_accessed=14 * MIB, transcendentals=0),
    )(place, *in_pieces, *down_pieces)


def halves(steps, sets):
    return [lambda d, number=number: jnp.clip(d - number * steps, 0, steps - 1) for number in range(sets)]


def expert_out_kernel(sets, steps, down_ref, *refs):
    out_ref = refs[sets]
    for number in range(sets):

        @pl.when(pl.program_id(0) // steps == number)
        def _():
            blocks, slots, _ = refs[number].shape
            weighted = refs[number][...].reshape(blocks * slots, FFE)
            for c in range(down_ref.shape[0]):
                slot_out = dot(weighted, down_ref[c]).astype(jnp.bfloat16)
                out_ref[:, c, 0] = slot_out.reshape(blocks, slots, -1)


def expert_outputs(weighted, weights_down):
    dl_n, slots, _ = weighted[0].shape
    col_n, _, width = weights_down.shape
    sets = len(weighted)
    blocks = 2 if dl_n % 2 == 0 else 1
    steps = dl_n // blocks
    return pl.pallas_call(
        functools.partial(expert_out_kernel, sets, steps),
        grid=(sets * steps,),
        in_specs=[pl.BlockSpec(weights_down.shape, lambda d: (0, 0, 0))]
        + [
            pl.BlockSpec((blocks, slots, FFE), lambda d, at=at: (at(d), 0, 0)) for at in halves(steps, sets)
        ],
        out_specs=pl.BlockSpec(
            (blocks, col_n, 1, slots, width), lambda d: (lax.rem(d, steps), 0, d // steps, 0, 0)
        ),
        out_shape=jax.ShapeDtypeStruct((dl_n, col_n, sets, slots, width), jnp.bfloat16),
        compiler_params=pltpu.CompilerParams(vmem_limit_bytes=40 * MIB),
        cost_estimate=pl.CostEstimate(
            flops=2 * sets * dl_n * slots * D * FFE, bytes_accessed=14 * MIB, transcendentals=0
        ),
    )(weights_down, *weighted)


def expert_grad_kernel(row_n, sets, steps, *refs):
    part = FFE // row_n
    step = pl.program_id(1)
    in_grad_ref, down_grad_ref, in_acc, down_acc = refs[4 * sets :]

    @pl.when(step == 0)
    def _():
        in_acc[...] = jnp.zeros_like(in_acc)
        down_acc[...] = jnp.zeros_like(down_acc)

    for number in range(sets):
        rows_ref, grads_ref, weighted_ref, pair_ref = refs[4 * number : 4 * number + 4]

        @pl.when(step // steps == number)
        def _():
            blocks, _, slots, width = rows_ref.shape
            weighted = weighted_ref[...].reshape(blocks * slots, FFE)
            pair = pair_ref[...].reshape(blocks * slots, 2 * FFE)
            rows = rows_ref[...].reshape(blocks * slots, width)
            grads = grads_ref[...].reshape(blocks * slots, width)
            in_acc[...] += dot(rows, pair, 0, 0)
            down_acc[...] += dot(weighted, grads, 0, 0)

    @pl.when(step == sets * steps - 1)
    def _():
        for r in range(row_n):
            for g in range(2):
                lanes = slice(g * FFE + r * part, g * FFE + (r + 1) * part)
                in_grad_ref[r, 0, g] = in_acc[:, lanes].astype(jnp.bfloat16)
            down_grad_ref[r, 0] = down_acc[r * part : (r + 1) * part, :].astype(jnp.bfloat16)


def expert_grads(sources, row_n):
    dl_n, col_n, slots, width = sources[0][0].shape
    sets = len(sources)
    blocks = 2 if dl_n % 2 == 0 else 1
    steps = dl_n // blocks
    part = FFE // row_n
    in_specs = []
    for at in halves(steps, sets):
        block = pl.BlockSpec((blocks, 1, slots, width), lambda c, d, at=at: (at(d), c, 0, 0))
        in_specs += [
            block,
            block,
            pl.BlockSpec((blocks, slots, FFE), lambda c, d, at=at: (at(d), 0, 0)),
            pl.BlockSpec((blocks, slots, 2 * FFE), lambda c, d, at=at: (at(d), 0, 0)),
        ]
    return pl.pallas_call(
        functools.partial(expert_grad_kernel, row_n, sets, steps),
        grid=(col_n, sets * steps),
        in_specs=in_specs,
        out_specs=[
            pl.BlockSpec((row_n, 1, 2, width, part), lambda c, d: (0, c, 0, 0, 0)),
            pl.BlockSpec((row_n, 1, part, width), lambda c, d: (0, c, 0, 0)),
        ],
        out_shape=[
            jax.ShapeDtypeStruct((row_n, col_n, 2, width, part), jnp.bfloat16),
            jax.ShapeDtypeStruct((row_n, col_n, part, width), jnp.bfloat16),
        ],
        scratch_shapes=[
            pltpu.VMEM((width, 2 * FFE), jnp.float32),
            pltpu.VMEM((FFE, width), jnp.float32),
        ],
        compiler_params=pltpu.CompilerParams(vmem_limit_bytes=58 * MIB),
        cost_estimate=pl.CostEstimate(
            flops=6 * sets * dl_n * slots * D * FFE, bytes_accessed=50 * MIB, transcendentals=0
        ),
    )(*[array for source in sources for array in source])


def adam_step(master, moment_one, moment_two, gradient, rate, decay):
    first = BETA_ONE * moment_one + (1.0 - BETA_ONE) * gradient
    second = BETA_TWO * moment_two + (1.0 - BETA_TWO) * gradient * gradient
    first_hat = first / (1.0 - BETA_ONE**STEP)
    second_hat = second / (1.0 - BETA_TWO**STEP)
    updated = master - rate * (first_hat / (jnp.sqrt(second_hat) + ADAM_EPS) + decay * master)
    return (updated, first, second)


def on_device(
    tokens,
    cotangent,
    routes,
    route_gates,
    block_ids,
    w_qkv,
    w_out,
    w_gate_up,
    w_down,
    gains,
    gain_first,
    gain_second,
    qkv_master,
    qkv_first,
    qkv_second,
    out_master,
    out_first,
    out_second,
    gate_up_master,
    gate_up_first,
    gate_up_second,
    down_master,
    down_first,
    down_second,
):
    dh_n, dl_n, row_n, col_n = (lax.axis_size(name) for name in ("dh", "dl", "row", "col"))
    dh_i, dl_i, row_i, col_i = (lax.axis_index(name) for name in ("dh", "dl", "row", "col"))
    dp_n = dh_n * dl_n
    grid_n = row_n * col_n
    width = w_qkv.shape[0]
    token_block = routes.shape[1]
    capacity = 5 * token_block * TOP // (4 * E)
    tokens_row = token_block // row_n
    seqs_row = tokens_row // LEN
    assert seqs_row * KVH == col_n and KVH == row_n
    seq_i, group_i = col_i // KVH, col_i % KVH
    experts_dp = E // dp_n
    share = grid_n // experts_dp
    assert share * experts_dp == grid_n
    slots = capacity // share
    low = jnp.bfloat16

    def far_pairs():
        return [(i, dh_n - 1 - i) for i in range(dh_n)]

    def from_far(values):
        both = lax.all_gather(values, "dh", axis=0)
        return lax.dynamic_index_in_dim(both, dh_n - 1 - dh_i, 0, False)

    def ring(values, axis):
        count = lax.axis_size(axis)
        moved = [values]
        for k in range(1, count):
            moved.append(lax.ppermute(values, axis, [(i, (i - k) % count) for i in range(count)]))
        return moved

    def row_blocks(values):
        return jnp.concatenate(ring(values, "row"), axis=0)

    inputs = tokens.reshape(tokens_row, width).astype(jnp.float32)
    qkv_row = lax.all_gather(w_qkv.reshape(width, -1), "row", axis=0)
    factor_one = lax.rsqrt(col_total(inputs * inputs) / D + EPS_NORM)
    far_routes = lax.ppermute(routes, "dh", far_pairs())
    far_gates = lax.ppermute(route_gates, "dh", far_pairs())
    ids = jnp.concatenate(ring(block_ids, "col"), axis=0)
    normed_one = (inputs * factor_one[:, None] * gains[0][None, :]).astype(low)
    normed_one = after(normed_one, far_routes, far_gates, ids)
    terms = jnp.einsum(
        "stf,gfh->sgth",
        normed_one.reshape(seqs_row, LEN, width),
        qkv_row,
        preferred_element_type=jnp.float32,
    )
    terms = terms.astype(low).reshape(col_n * LEN, -1)
    packed = lax.psum_scatter(terms, "col", scatter_dimension=0, tiled=True)

    ids = lax.dynamic_index_in_dim(ids, (row_i * seqs_row + seq_i - col_i) % col_n, 0, False)

    ranks, gates = slot_ranks(routes, route_gates)
    far_ranks, far_gates = slot_ranks(far_routes, far_gates)
    offsets = (jnp.arange(share) * slots).astype(jnp.int32)

    def unit_grid(values):
        values = values.reshape(dh_n, dl_n, row_n, col_n, token_block)
        return jnp.roll(values, -row_i * tokens_row, axis=-1)

    def unit_slots(ranks):
        return unit_grid(ranks[:, None, :] - offsets[None, :, None])

    def near(values):
        values = lax.dynamic_index_in_dim(values, dh_i, 0, False)
        return lax.dynamic_index_in_dim(values, row_i, 1, False)

    def here(values):
        return lax.dynamic_index_in_dim(values, col_i, 1, False)

    def unit_gates(gates):
        return here(near(unit_grid(jnp.broadcast_to(gates[:, None, :], (E, share, token_block)))))

    all_ranks = unit_slots(ranks)
    unit_ranks = [near(all_ranks), near(unit_slots(far_ranks))]
    here_ranks = [here(values) for values in unit_ranks]
    here_gates = [unit_gates(gates), unit_gates(far_gates)]

    def hot(number, start=0, count=token_block):
        chosen = unit_ranks[number][:, :, None, start : start + count]
        return chosen == jnp.arange(slots, dtype=jnp.int32)[None, None, :, None]

    def dispatch(number, rows):
        picked = jnp.einsum(
            "dcst,tf->dcsf", hot(number).astype(low), rows, preferred_element_type=jnp.float32
        )
        return picked.astype(low).reshape(dl_n * col_n, slots, width)

    def to_experts(values):
        return to_owners(values, ("dl", "col")).reshape(dl_n, col_n, slots, width)

    def token_sums(number, values):
        values = values.reshape(dl_n, col_n, slots, width)
        total = None
        for k in range(1, row_n):
            chosen = hot(number, k * tokens_row, tokens_row).astype(low)
            part = jnp.einsum("dcst,dcsf->tf", chosen, values, preferred_element_type=jnp.float32)
            values = after(values, part)
            part = lax.ppermute(part, "row", [(i, (i + k) % row_n) for i in range(row_n)])
            total = part if total is None else total + part
        chosen = hot(number, 0, tokens_row).astype(low)
        own = jnp.einsum("dcst,dcsf->tf", chosen, values, preferred_element_type=jnp.float32)
        return own + total

    def here_hot(number):
        return here_ranks[number][:, None, :] == jnp.arange(slots, dtype=jnp.int32)[None, :, None]

    slot_gate = jnp.stack(
        [
            jnp.sum(jnp.where(here_hot(number), here_gates[number][:, None, :], 0.0), axis=-1)
            for number in range(2)
        ],
        axis=1,
    )

    start = (dh_i * dl_n + dl_i) * experts_dp
    experts_in = jnp.swapaxes(lax.dynamic_slice_in_dim(w_gate_up, start, experts_dp, 0), 1, 2)
    in_pieces, down_pieces, piece_pairs = [], [], []
    for k in range(grid_n):
        kr, kc = k // col_n, k % col_n
        target = (((row_i - kr) % row_n) * col_n + (col_i - kc) % col_n) // share
        in_pieces.append(lax.dynamic_index_in_dim(experts_in, target, 0, False))
        down_pieces.append(lax.dynamic_index_in_dim(w_down, start + target, 0, False))
        piece_pairs.append(
            [
                (r * col_n + c, ((r - kr) % row_n) * col_n + (c - kc) % col_n)
                for r in range(row_n)
                for c in range(col_n)
            ]
        )

    grad_rows = cotangent.reshape(tokens_row, width)
    grad_low = grad_rows.astype(low)
    far_low = to_owners(jnp.broadcast_to(grad_low, (dh_n,) + grad_low.shape), "dh")

    def all_features(values):
        values = jnp.roll(jnp.stack(ring(values, "col")), col_i, axis=0)
        return values

    def all_rows(values):
        return jnp.concatenate(ring(values, "row"), axis=1)

    def dispatch_wide(number, rows):
        picked = jnp.einsum(
            "dst,ctf->dcsf", here_hot(number).astype(low), rows, preferred_element_type=jnp.float32
        )
        return picked.astype(low)

    own_wide = ring(after(grad_low, factor_one), "col")
    own_wide[-1] = after(own_wide[-1], terms, slot_gate, *here_ranks, *unit_ranks)
    own_wide = jnp.roll(jnp.stack(own_wide), col_i, axis=0)
    own_picked = dispatch_wide(0, all_rows(own_wide))
    own_grads = to_owners(after(own_picked, far_low), "dl")
    my_gate = to_owners(after(slot_gate, own_grads), "dl")
    my_gate = jnp.swapaxes(my_gate, 0, 1)[..., None]
    far_low = lax.dynamic_index_in_dim(far_low, dh_n - 1 - dh_i, 0, False)
    far_wide = all_features(far_low)

    packed = after(packed, own_picked)
    mixed, log_total, tops = attend_forward(packed, ids)
    heads = lax.all_gather(mixed, "col", axis=0)
    heads = after(heads, own_grads, *in_pieces, *down_pieces).reshape(seqs_row, KVH, LEN, GROUP * HD)
    out_row = lax.all_gather(after(w_out[0], packed), "row", axis=0)
    attn = jnp.einsum("sgth,ghf->stf", heads, out_row, preferred_element_type=jnp.float32)
    hidden = inputs + attn.reshape(tokens_row, width)

    factor_two = lax.rsqrt(col_total(hidden * hidden) / D + EPS_NORM)
    normed_two = (hidden * factor_two[:, None] * gains[1][None, :]).astype(low)
    far_two = from_far(normed_two)
    far_picked = dispatch_wide(1, all_rows(after(far_wide, normed_two)))
    far_grads = to_owners(after(far_picked, my_gate), "dl")

    def spread(piece, pairs):
        return lax.ppermute(after(piece, normed_two), ("row", "col"), pairs)

    for k in range(1, grid_n):
        down_pieces[k] = spread(down_pieces[k], piece_pairs[k])
        in_pieces[k] = spread(in_pieces[k], piece_pairs[k])
    weights_in, weights_down = join_weights(
        in_pieces, down_pieces, jnp.stack([row_i, col_i]).astype(jnp.int32), row_n, col_n
    )
    far_two = after(far_two, weights_in)
    far_slots = dispatch(1, row_blocks(far_two))
    far_rows = to_experts(after(far_slots, far_grads))
    own_slots = dispatch(0, after(row_blocks(normed_two), far_slots))
    own_rows = to_experts(after(own_slots, far_rows))

    far_back, far_weighted, far_pair = expert_passes(
        far_rows, far_grads, my_gate[1], weights_in, weights_down
    )
    own_back, own_weighted, own_pair = expert_passes(
        after(own_rows, far_back), own_grads, my_gate[0], weights_in, weights_down
    )

    def send_back(values):
        return to_owners(values.reshape(dl_n * col_n, slots, width), ("dl", "col"))

    far_back = send_back(after(far_back, own_rows))
    slot_out = expert_outputs([own_weighted, far_weighted], weights_down)
    own_back = send_back(after(own_back, far_back))
    far_sums = token_sums(1, after(far_back, slot_out)).astype(low)
    in_grad, down_grad = expert_grads(
        [
            (own_rows, own_grads, after(own_weighted, far_sums), own_pair),
            (far_rows, far_grads, far_weighted, far_pair),
        ],
        row_n,
    )
    far_sums = from_far(far_sums)
    own_back = after(own_back, in_grad)
    own_sums = token_sums(0, own_back)
    grad_normed_two = own_sums + far_sums.astype(jnp.float32)
    slot_out = to_owners(after(slot_out, own_back).reshape((dl_n * col_n,) + slot_out.shape[2:]), ("dl", "col"))

    def block_grads(grads):
        grads = to_owners(grads.reshape((grid_n,) + grads.shape[2:]), ("row", "col"))
        if share > 1:
            grads = grads.astype(jnp.float32)
            grads = jnp.sum(grads.reshape((experts_dp, share) + grads.shape[1:]), axis=1)
        return grads

    grad_hidden_norm, grad_gain_two = norm_backward(hidden, factor_two, gains[1], grad_normed_two)
    grad_hidden = grad_rows + grad_hidden_norm
    grad_attn = grad_hidden.astype(low)
    terms = jnp.einsum(
        "stf,ghf->sgth",
        grad_attn.reshape(seqs_row, LEN, width),
        out_row,
        preferred_element_type=jnp.float32,
    )
    terms = terms.astype(low).reshape(col_n * LEN, -1)
    grad_heads = lax.psum_scatter(terms, "col", scatter_dimension=0, tiled=True)
    full_top = jnp.full((KVH, GROUP), -1e30, jnp.float32)
    full_top = lax.dynamic_update_slice(
        full_top, jnp.max(tops, axis=(1, 2))[None], (group_i, jnp.zeros((), jnp.int32))
    )
    own_out, far_out = slot_out[:, 0], slot_out[:, 1]
    far_out_sums = token_sums(1, after(far_out, terms)).astype(low)
    down_grad = after(down_grad, grad_heads)
    grad_heads = after(grad_heads, far_out_sums)
    grad_packed = attend_backward(packed, ids, log_total, grad_heads)
    packed_all = lax.all_gather(grad_packed, "col", axis=0).reshape(seqs_row, KVH, LEN, -1)

    own_out_sums = token_sums(0, after(own_out, grad_packed))
    packed_all = after(packed_all, own_out_sums)
    far_out_sums = lax.ppermute(far_out_sums, "dh", far_pairs())
    block_output = hidden + own_out_sums + far_out_sums.astype(jnp.float32)

    def owner_sums(left, right):
        columns = right.shape[-1]

        def term(k):
            group = lax.dynamic_index_in_dim(right, (row_i + k) % row_n, 1, False)
            return jnp.einsum("stf,sth->fh", left, group, preferred_element_type=jnp.float32)

        total = None
        for k in range(1, row_n):
            part = term(k)
            left = after(left, part)
            part = lax.ppermute(part, "row", [(i, (i + k) % row_n) for i in range(row_n)])
            total = part if total is None else total + part
        total = (term(0) + total).astype(low)
        total = to_owners(total, ("dh", "dl")).reshape(dp_n, -1, columns)
        return jnp.sum(total.astype(jnp.float32), axis=0)

    grad_normed_one = jnp.einsum(
        "sgth,gfh->stf", packed_all, qkv_row, preferred_element_type=jnp.float32
    ).reshape(tokens_row, width)
    grad_out = owner_sums(grad_attn.reshape(seqs_row, LEN, width), after(heads, grad_heads))
    grad_gate_up = block_grads(after(in_grad, packed_all))
    grad_qkv = owner_sums(normed_one.reshape(seqs_row, LEN, width), packed_all)
    grad_down = block_grads(down_grad)
    grad_gate_up = jnp.swapaxes(grad_gate_up, 1, 2)
    grad_gate_up = with_layout_constraint(grad_gate_up, Layout((0, 1, 2, 3)))
    grad_out, grad_qkv = grad_out.T[None], grad_qkv[:, None]
    grad_input_norm, grad_gain_one = norm_backward(inputs, factor_one, gains[0], grad_normed_one)
    input_grad = grad_hidden + grad_input_norm

    full_top = butterfly(after(full_top, packed_all), jnp.maximum, ("col",))

    tops_row = jnp.pad(full_top.reshape(1, -1), ((0, 0), (0, width - KVH * GROUP)))
    small = jnp.concatenate([grad_gain_one[None], grad_gain_two[None], tops_row])

    def combine(left, right):
        return jnp.concatenate([left[:2] + right[:2], jnp.maximum(left[2:], right[2:])])

    small = butterfly(small, combine, ("row", "dh", "dl"))
    grad_gains, head_top = small[:2], small[2, : KVH * GROUP].reshape(KVH, GROUP)

    factors = TAU_CLIP / jnp.maximum(head_top, TAU_CLIP)
    local_factors = lax.dynamic_slice_in_dim(factors, row_i, 1, 0)
    query_scale = jnp.repeat(jnp.sqrt(local_factors), HD, axis=1)
    key_scale = jnp.repeat(jnp.sqrt(jnp.min(local_factors, axis=1, keepdims=True)), HD, axis=1)
    column_scale = jnp.concatenate([query_scale, key_scale, jnp.ones_like(key_scale)], axis=1)
    qkv_new, qkv_one, qkv_two = adam_step(
        qkv_master, qkv_first, qkv_second, grad_qkv, D ** (-0.5), DECAY_RATE
    )
    qkv_new = qkv_new * column_scale[None]
    out_new, out_one, out_two = adam_step(
        out_master, out_first, out_second, grad_out, max(D // 192, 1) ** (-0.5), DECAY_RATE
    )
    gate_up_new, gate_up_one, gate_up_two = adam_step(
        gate_up_master, gate_up_first, gate_up_second, grad_gate_up, D ** (-0.5), DECAY_RATE
    )
    down_new, down_one, down_two = adam_step(
        down_master, down_first, down_second, grad_down, FFE ** (-0.5), DECAY_RATE
    )
    gains_new, gains_one, gains_two = adam_step(
        gains, gain_first, gain_second, grad_gains, 0.2, 0.0
    )
    return (
        block_output.reshape(1, -1, 2 * width),
        input_grad.reshape(1, -1, 2 * width),
        qkv_new,
        qkv_one,
        qkv_two,
        qkv_new.astype(jnp.bfloat16),
        out_new,
        out_one,
        out_two,
        out_new.astype(jnp.bfloat16),
        gate_up_new,
        gate_up_one,
        gate_up_two,
        gate_up_new.astype(jnp.bfloat16),
        down_new,
        down_one,
        down_two,
        down_new.astype(jnp.bfloat16),
        gains_new,
        gains_one,
        gains_two,
        factors.reshape(-1),
    )


def solution(mesh):
    devices = mesh.devices
    devices = devices.reshape((2, devices.shape[0] // 2) + devices.shape[1:])
    mesh = jax.sharding.Mesh(devices, ("dh", "dl", "row", "col"))
    dp = ("dh", "dl")
    in_specs = (
        P("col", (*dp, "row"), None),
        P("col", (*dp, "row"), None),
        P(None, dp),
        P(None, dp),
        P((*dp, "col"), None),
        P("col", "row", None),
        P("row", None, "col"),
        P(None, "col", None, "row"),
        P(None, "row", "col"),
        P(None, "col"),
        P(None, "col"),
        P(None, "col"),
        P(("col", *dp), "row", None),
        P(("col", *dp), "row", None),
        P(("col", *dp), "row", None),
        P("row", None, ("col", *dp)),
        P("row", None, ("col", *dp)),
        P("row", None, ("col", *dp)),
        P(dp, "col", None, "row"),
        P(dp, "col", None, "row"),
        P(dp, "col", None, "row"),
        P(dp, "row", "col"),
        P(dp, "row", "col"),
        P(dp, "row", "col"),
    )
    out_specs = (
        P("col", (*dp, "row"), None),
        P("col", (*dp, "row"), None),
        P(("col", *dp), "row", None),
        P(("col", *dp), "row", None),
        P(("col", *dp), "row", None),
        P(("col", *dp), "row", None),
        P("row", None, ("col", *dp)),
        P("row", None, ("col", *dp)),
        P("row", None, ("col", *dp)),
        P("row", None, ("col", *dp)),
        P(dp, "col", None, "row"),
        P(dp, "col", None, "row"),
        P(dp, "col", None, "row"),
        P(dp, "col", None, "row"),
        P(dp, "row", "col"),
        P(dp, "row", "col"),
        P(dp, "row", "col"),
        P(dp, "row", "col"),
        P(None, "col"),
        P(None, "col"),
        P(None, "col"),
        P(),
    )
    return jax.shard_map(
        on_device, mesh=mesh, in_specs=in_specs, out_specs=out_specs, check_vma=False
    )
```

```python
import functools

import jax
import jax.numpy as jnp
from jax import lax
from jax.experimental import pallas as pl
from jax.experimental.layout import Layout, with_layout_constraint
from jax.experimental.pallas import tpu as pltpu
from jax.sharding import PartitionSpec as P

D = 1536
KVH = 2
HD = 128
E = 32
FFE = 768
TOP = 4
GROUP = 6
LEN = 1024
STEP = 5


EPS_NORM = 1e-06
BETA_ONE = 0.5
BETA_TWO = 0.5
ADAM_EPS = 1e-08
DECAY_RATE = 0.1
TAU_CLIP = 3.0


QUERIES = 256
MIB = 1 << 20
NO_COST = pl.CostEstimate(flops=0, bytes_accessed=0, transcendentals=0)


def dot(left, right, left_dim=1, right_dim=0):
    return lax.dot_general(
        left, right, (((left_dim,), (right_dim,)), ((), ())), preferred_element_type=jnp.float32
    )


def pass_on(*refs):
    pass


def after(values, *earlier):
    return pl.pallas_call(
        pass_on,
        in_specs=[pl.BlockSpec(memory_space=pl.ANY)] * (1 + len(earlier)),
        out_specs=pl.BlockSpec(memory_space=pl.ANY),
        out_shape=jax.ShapeDtypeStruct(values.shape, values.dtype),
        input_output_aliases={0: 0},
        cost_estimate=NO_COST,
    )(values, *earlier)


def col_total(values):
    return lax.psum(jnp.sum(values, axis=1), "col")


def butterfly(values, combine, axes):
    for axis in axes:
        count = lax.axis_size(axis)
        bit = 1
        while bit < count:
            pairs = [(i, i ^ bit) for i in range(count)]
            values = combine(values, lax.ppermute(values, axis, pairs))
            bit *= 2
    return values


def norm_backward(values, factor, gain, grad_normed):
    inner = col_total(values * gain[None, :] * grad_normed) / D
    grad_values = (
        factor[:, None] * gain[None, :] * grad_normed - values * (factor**3 * inner)[:, None]
    )
    grad_gain = jnp.sum(grad_normed * values * factor[:, None], axis=0)
    return (grad_values, grad_gain)


def to_owners(values, axes):
    return lax.all_to_all(values, axes, split_axis=0, concat_axis=0, tiled=True)


def slot_ranks(routes, route_gates):
    tokens = routes.shape[1]
    hits = routes[:, None, :] == jnp.arange(E, dtype=jnp.int32)[None, :, None]
    gates = jnp.sum(jnp.where(hits, route_gates[:, None, :], 0.0), axis=0)
    chosen = jnp.any(hits, axis=0)
    lanes = jnp.arange(128)
    upto = (lanes[:, None] <= lanes[None, :]).astype(jnp.bfloat16)
    runs = jnp.einsum(
        "ebt,ts->ebs",
        chosen.reshape(E, tokens // 128, 128).astype(jnp.bfloat16),
        upto,
        preferred_element_type=jnp.float32,
    ).astype(jnp.int32)
    totals = runs[:, :, -1]
    ranks = (runs + (jnp.cumsum(totals, axis=1) - totals)[:, :, None]).reshape(E, tokens) - 1
    return (jnp.where(chosen, ranks, -1), gates)


def key_reach(chunk):
    return min((chunk + 2) * QUERIES, LEN)


def scores_turned(queries, keys, id_row, id_col):
    scores = dot(keys, queries, 1, 1) * HD ** (-0.5)
    return jnp.where(id_col <= id_row, scores, -1e30)


def attend_kernel(query_ref, key_ref, value_ref, id_row_ref, id_col_ref, mixed_ref, log_ref, top_ref):
    value_turned = value_ref[...].T
    for chunk in range(LEN // QUERIES):
        rows = slice(chunk * QUERIES, (chunk + 1) * QUERIES)
        reach = key_reach(chunk)
        masked = scores_turned(
            query_ref[rows, :], key_ref[:reach, :], id_row_ref[:, rows], id_col_ref[:reach, :]
        )
        top = jnp.max(masked, axis=0, keepdims=True)
        weights = jnp.exp(masked - top)
        total = jnp.sum(weights, axis=0, keepdims=True)
        probs = (weights * (1.0 / total)).astype(jnp.bfloat16)
        mixed_ref[rows, :] = dot(value_turned[:, :reach], probs).T.astype(jnp.bfloat16)
        log_ref[0, :, rows] = top + jnp.log(total)
        top_ref[0, :, rows] = top


def attend_forward(packed, blocks):
    head = pl.BlockSpec((LEN, HD), lambda h: (0, h))
    row = pl.BlockSpec((1, 1, LEN), lambda h: (h, 0, 0))
    return pl.pallas_call(
        attend_kernel,
        grid=(GROUP,),
        in_specs=[
            head,
            pl.BlockSpec((LEN, HD), lambda h: (0, GROUP)),
            pl.BlockSpec((LEN, HD), lambda h: (0, GROUP + 1)),
            pl.BlockSpec((1, LEN), lambda h: (0, 0)),
            pl.BlockSpec((LEN, 1), lambda h: (0, 0)),
        ],
        out_specs=[head, row, row],
        out_shape=[
            jax.ShapeDtypeStruct((LEN, GROUP * HD), jnp.bfloat16),
            jax.ShapeDtypeStruct((GROUP, 1, LEN), jnp.float32),
            jax.ShapeDtypeStruct((GROUP, 1, LEN), jnp.float32),
        ],
        compiler_params=pltpu.CompilerParams(vmem_limit_bytes=40 * MIB),
        cost_estimate=NO_COST,
    )(packed, packed, packed, blocks[None, :], blocks[:, None])


def attend_back_kernel(
    query_ref, key_ref, value_ref, grad_ref, log_ref, id_row_ref, id_col_ref, out_ref, keys_acc, values_acc
):
    head = pl.program_id(0)

    @pl.when(head == 0)
    def _():
        keys_acc[...] = jnp.zeros_like(keys_acc)
        values_acc[...] = jnp.zeros_like(values_acc)

    key_turned = key_ref[...].T
    for chunk in range(LEN // QUERIES):
        rows = slice(chunk * QUERIES, (chunk + 1) * QUERIES)
        reach = key_reach(chunk)
        queries = query_ref[rows, :]
        grads = grad_ref[rows, :]
        masked = scores_turned(queries, key_ref[:reach, :], id_row_ref[:, rows], id_col_ref[:reach, :])
        probs = jnp.exp(masked - log_ref[0, :, rows])
        grad_probs = dot(value_ref[:reach, :], grads, 1, 1)
        delta = jnp.sum(probs * grad_probs, axis=0, keepdims=True)
        grad_scores = (probs * (grad_probs - delta)).astype(jnp.bfloat16)
        values_acc[:reach, :] += dot(probs.astype(jnp.bfloat16), grads)
        keys_acc[:reach, :] += dot(grad_scores, queries)
        grad_query = dot(key_turned[:, :reach], grad_scores).T * HD ** (-0.5)
        lanes = pl.ds(pl.multiple_of(head * HD, HD), HD)
        out_ref[rows, lanes] = grad_query.astype(jnp.bfloat16)

    @pl.when(head == GROUP - 1)
    def _():
        out_ref[:, GROUP * HD : (GROUP + 1) * HD] = (keys_acc[...] * HD ** (-0.5)).astype(jnp.bfloat16)
        out_ref[:, (GROUP + 1) * HD :] = values_acc[...].astype(jnp.bfloat16)


def attend_backward(packed, blocks, log_total, grad_heads):
    head = pl.BlockSpec((LEN, HD), lambda h: (0, h))
    return pl.pallas_call(
        attend_back_kernel,
        grid=(GROUP,),
        in_specs=[
            head,
            pl.BlockSpec((LEN, HD), lambda h: (0, GROUP)),
            pl.BlockSpec((LEN, HD), lambda h: (0, GROUP + 1)),
            head,
            pl.BlockSpec((1, 1, LEN), lambda h: (h, 0, 0)),
            pl.BlockSpec((1, LEN), lambda h: (0, 0)),
            pl.BlockSpec((LEN, 1), lambda h: (0, 0)),
        ],
        out_specs=pl.BlockSpec((LEN, (GROUP + 2) * HD), lambda h: (0, 0)),
        out_shape=jax.ShapeDtypeStruct((LEN, (GROUP + 2) * HD), jnp.bfloat16),
        scratch_shapes=[pltpu.VMEM((LEN, HD), jnp.float32)] * 2,
        compiler_params=pltpu.CompilerParams(vmem_limit_bytes=40 * MIB),
        cost_estimate=NO_COST,
    )(packed, packed, packed, grad_heads, log_total, blocks[None, :], blocks[:, None])


def pick_kernel(ranks_ref, *refs):
    blocks, out_ref = refs[:-1], refs[-1]
    _, cols, slots, _ = out_ref.shape
    rows = len(blocks) // cols
    count = blocks[0].shape[0]
    slot = lax.broadcasted_iota(jnp.int32, (slots, rows * count), 0)
    hot = (ranks_ref[0] == slot).astype(jnp.float32).astype(jnp.bfloat16)
    for c in range(cols):
        picked = dot(hot[:, :count], blocks[c][...])
        for k in range(1, rows):
            picked += dot(hot[:, k * count : (k + 1) * count], blocks[k * cols + c][...])
        out_ref[0, c] = picked.astype(jnp.bfloat16)


def pick_slots(ranks, slots, blocks):
    units, count = ranks.shape
    cols = len(blocks[0])
    flat = [block for row in blocks for block in row]
    width = flat[0].shape[1]
    whole = pl.BlockSpec(flat[0].shape, lambda u: (0, 0), pipeline_mode=pl.Buffered(1))
    return pl.pallas_call(
        pick_kernel,
        grid=(units,),
        in_specs=[pl.BlockSpec((1, 1, count), lambda u: (u, 0, 0))] + [whole] * len(flat),
        out_specs=pl.BlockSpec((1, cols, slots, width), lambda u: (u, 0, 0, 0)),
        out_shape=jax.ShapeDtypeStruct((units, cols, slots, width), jnp.bfloat16),
        compiler_params=pltpu.CompilerParams(vmem_limit_bytes=56 * MIB),
        cost_estimate=NO_COST,
    )(ranks[:, None, :], *flat)


def expert_kernel(col_n, place_ref, rows_ref, grads_ref, gate_ref, in_ref, down_ref, back_ref, weighted_ref, pair_ref):
    gate_up = dot(rows_ref[0, 0], in_ref[0])
    grad_weighted = dot(grads_ref[0, 0], down_ref[place_ref[1]], 1, 1)
    for c in range(1, col_n):
        gate_up += dot(rows_ref[0, c], in_ref[c])
        grad_weighted += dot(grads_ref[0, c], down_ref[lax.rem(place_ref[1] + c, col_n)], 1, 1)
    gate_half, up_half, scale = gate_up[:, :FFE], gate_up[:, FFE:], gate_ref[0]
    sigmoid_gate = jax.nn.sigmoid(gate_half)
    silu_gate = gate_half * sigmoid_gate
    weighted_ref[0] = (silu_gate * up_half * scale).astype(jnp.bfloat16)
    grad_act = grad_weighted * scale
    grad_gate = grad_act * up_half * sigmoid_gate * (1.0 + gate_half * (1.0 - sigmoid_gate))
    pair_ref[0, :, :FFE] = grad_gate.astype(jnp.bfloat16)
    pair_ref[0, :, FFE:] = (grad_act * silu_gate).astype(jnp.bfloat16)
    for c in range(col_n):
        back_ref[0, c] = dot(pair_ref[0], in_ref[c], 1, 1).astype(jnp.bfloat16)


def expert_passes(place, slot_rows, slot_grads, gates, weights_in, weights_down):
    dl_n, col_n, slots, width = slot_rows.shape
    block = pl.BlockSpec((1, col_n, slots, width), lambda d: (d, 0, 0, 0))
    return pl.pallas_call(
        functools.partial(expert_kernel, col_n),
        grid=(dl_n,),
        in_specs=[
            pl.BlockSpec(memory_space=pltpu.SMEM),
            block,
            block,
            pl.BlockSpec((1, slots, 1), lambda d: (d, 0, 0)),
            pl.BlockSpec(weights_in.shape, lambda d: (0, 0, 0)),
            pl.BlockSpec(weights_down.shape, lambda d: (0, 0, 0)),
        ],
        out_specs=[
            block,
            pl.BlockSpec((1, slots, FFE), lambda d: (d, 0, 0)),
            pl.BlockSpec((1, slots, 2 * FFE), lambda d: (d, 0, 0)),
        ],
        out_shape=[
            jax.ShapeDtypeStruct(slot_rows.shape, jnp.bfloat16),
            jax.ShapeDtypeStruct((dl_n, slots, FFE), jnp.bfloat16),
            jax.ShapeDtypeStruct((dl_n, slots, 2 * FFE), jnp.bfloat16),
        ],
        compiler_params=pltpu.CompilerParams(vmem_limit_bytes=56 * MIB),
        cost_estimate=NO_COST,
    )(place, slot_rows, slot_grads, gates, weights_in, weights_down)


def join_kernel(row_n, col_n, place_ref, *refs):
    count = row_n * col_n
    in_refs, down_refs, (in_out, down_out) = refs[:count], refs[count : 2 * count], refs[2 * count :]
    part = FFE // row_n
    for k in range(count):
        r = lax.rem(place_ref[0] + k // col_n, row_n)
        c = lax.rem(place_ref[1] + k % col_n, col_n)
        for g in range(2):
            lanes = pl.ds(pl.multiple_of(g * FFE + r * part, 128), part)
            in_out[c, :, lanes] = in_refs[k][g]
        down_out[c, pl.ds(pl.multiple_of(r * part, 128), part), :] = down_refs[k][...]


def join_weights(in_pieces, down_pieces, place, row_n, col_n):
    width = in_pieces[0].shape[1]
    return pl.pallas_call(
        functools.partial(join_kernel, row_n, col_n),
        in_specs=[pl.BlockSpec(memory_space=pltpu.SMEM)]
        + [pl.BlockSpec(memory_space=pltpu.VMEM)] * (2 * row_n * col_n),
        out_specs=[pl.BlockSpec(memory_space=pltpu.VMEM)] * 2,
        out_shape=[
            jax.ShapeDtypeStruct((col_n, width, 2 * FFE), jnp.bfloat16),
            jax.ShapeDtypeStruct((col_n, FFE, width), jnp.bfloat16),
        ],
        compiler_params=pltpu.CompilerParams(vmem_limit_bytes=40 * MIB),
        cost_estimate=NO_COST,
    )(place, *in_pieces, *down_pieces)


def halves(steps, sets):
    return [lambda d, number=number: jnp.clip(d - number * steps, 0, steps - 1) for number in range(sets)]


def expert_out_kernel(sets, steps, down_ref, *refs):
    out_ref = refs[sets]
    for number in range(sets):

        @pl.when(pl.program_id(0) // steps == number)
        def _():
            blocks, slots, _ = refs[number].shape
            weighted = refs[number][...].reshape(blocks * slots, FFE)
            for c in range(down_ref.shape[0]):
                slot_out = dot(weighted, down_ref[c]).astype(jnp.bfloat16)
                out_ref[:, c, 0] = slot_out.reshape(blocks, slots, -1)


def expert_outputs(weighted, weights_down):
    dl_n, slots, _ = weighted[0].shape
    col_n, _, width = weights_down.shape
    sets = len(weighted)
    blocks = 2 if dl_n % 2 == 0 else 1
    steps = dl_n // blocks
    return pl.pallas_call(
        functools.partial(expert_out_kernel, sets, steps),
        grid=(sets * steps,),
        in_specs=[pl.BlockSpec(weights_down.shape, lambda d: (0, 0, 0))]
        + [
            pl.BlockSpec((blocks, slots, FFE), lambda d, at=at: (at(d), 0, 0)) for at in halves(steps, sets)
        ],
        out_specs=pl.BlockSpec(
            (blocks, col_n, 1, slots, width), lambda d: (lax.rem(d, steps), 0, d // steps, 0, 0)
        ),
        out_shape=jax.ShapeDtypeStruct((dl_n, col_n, sets, slots, width), jnp.bfloat16),
        compiler_params=pltpu.CompilerParams(vmem_limit_bytes=40 * MIB),
        cost_estimate=NO_COST,
    )(weights_down, *weighted)


def expert_grad_kernel(row_n, sets, steps, place_ref, *refs):
    part = FFE // row_n
    step = pl.program_id(1)
    in_grad_ref, down_grad_ref, in_acc, down_acc = refs[4 * sets :]

    @pl.when(step == 0)
    def _():
        in_acc[...] = jnp.zeros_like(in_acc)
        down_acc[...] = jnp.zeros_like(down_acc)

    for number in range(sets):
        rows_ref, grads_ref, weighted_ref, pair_ref = refs[4 * number : 4 * number + 4]

        @pl.when(step // steps == number)
        def _():
            blocks, _, slots, width = rows_ref.shape
            weighted = weighted_ref[...].reshape(blocks * slots, FFE)
            pair = pair_ref[...].reshape(blocks * slots, 2 * FFE)
            rows = rows_ref[...].reshape(blocks * slots, width)
            grads = grads_ref[...].reshape(blocks * slots, width)
            in_acc[...] += dot(rows, pair, 0, 0)
            down_acc[...] += dot(weighted, grads, 0, 0)

    @pl.when(step == sets * steps - 1)
    def _():
        for r in range(row_n):
            for g in range(2):
                lanes = slice(g * FFE + r * part, g * FFE + (r + 1) * part)
                in_grad_ref[r, 0, g] = in_acc[:, lanes].astype(jnp.bfloat16)
            down_grad_ref[r, 0] = down_acc[r * part : (r + 1) * part, :].astype(jnp.bfloat16)


def expert_grads(place, sources, row_n):
    dl_n, col_n, slots, width = sources[0][0].shape
    sets = len(sources)
    blocks = 2 if dl_n % 2 == 0 else 1
    steps = dl_n // blocks
    part = FFE // row_n
    in_specs = []
    for at in halves(steps, sets):
        in_specs += [
            pl.BlockSpec((blocks, 1, slots, width), lambda c, d, p, at=at: (at(d), c, 0, 0)),
            pl.BlockSpec(
                (blocks, 1, slots, width),
                lambda c, d, p, at=at: (at(d), lax.rem(c - p[1] + col_n, col_n), 0, 0),
            ),
            pl.BlockSpec((blocks, slots, FFE), lambda c, d, p, at=at: (at(d), 0, 0)),
            pl.BlockSpec((blocks, slots, 2 * FFE), lambda c, d, p, at=at: (at(d), 0, 0)),
        ]
    return pl.pallas_call(
        functools.partial(expert_grad_kernel, row_n, sets, steps),
        grid_spec=pltpu.PrefetchScalarGridSpec(
            num_scalar_prefetch=1,
            grid=(col_n, sets * steps),
            in_specs=in_specs,
            out_specs=[
                pl.BlockSpec((row_n, 1, 2, width, part), lambda c, d, p: (0, c, 0, 0, 0)),
                pl.BlockSpec((row_n, 1, part, width), lambda c, d, p: (0, c, 0, 0)),
            ],
            scratch_shapes=[
                pltpu.VMEM((width, 2 * FFE), jnp.float32),
                pltpu.VMEM((FFE, width), jnp.float32),
            ],
        ),
        out_shape=[
            jax.ShapeDtypeStruct((row_n, col_n, 2, width, part), jnp.bfloat16),
            jax.ShapeDtypeStruct((row_n, col_n, part, width), jnp.bfloat16),
        ],
        compiler_params=pltpu.CompilerParams(vmem_limit_bytes=58 * MIB),
        cost_estimate=NO_COST,
    )(place, *[array for source in sources for array in source])


def adam_step(master, moment_one, moment_two, gradient, rate, decay):
    first = BETA_ONE * moment_one + (1.0 - BETA_ONE) * gradient
    second = BETA_TWO * moment_two + (1.0 - BETA_TWO) * gradient * gradient
    first_hat = first / (1.0 - BETA_ONE**STEP)
    second_hat = second / (1.0 - BETA_TWO**STEP)
    updated = master - rate * (first_hat / (jnp.sqrt(second_hat) + ADAM_EPS) + decay * master)
    return (updated, first, second)


def on_device(
    tokens,
    cotangent,
    routes,
    route_gates,
    block_ids,
    w_qkv,
    w_out,
    w_gate_up,
    w_down,
    gains,
    gain_first,
    gain_second,
    qkv_master,
    qkv_first,
    qkv_second,
    out_master,
    out_first,
    out_second,
    gate_up_master,
    gate_up_first,
    gate_up_second,
    down_master,
    down_first,
    down_second,
):
    dh_n, dl_n, row_n, col_n = (lax.axis_size(name) for name in ("dh", "dl", "row", "col"))
    dh_i, dl_i, row_i, col_i = (lax.axis_index(name) for name in ("dh", "dl", "row", "col"))
    dp_n = dh_n * dl_n
    grid_n = row_n * col_n
    width = w_qkv.shape[0]
    token_block = routes.shape[1]
    capacity = 5 * token_block * TOP // (4 * E)
    tokens_row = token_block // row_n
    seqs_row = tokens_row // LEN
    assert seqs_row * KVH == col_n and KVH == row_n
    seq_i, group_i = col_i // KVH, col_i % KVH
    experts_dp = E // dp_n
    share = grid_n // experts_dp
    assert share * experts_dp == grid_n
    slots = capacity // share
    low = jnp.bfloat16

    def far_pairs():
        return [(i, dh_n - 1 - i) for i in range(dh_n)]

    def from_far(values):
        both = lax.all_gather(values, "dh", axis=0)
        return lax.dynamic_index_in_dim(both, dh_n - 1 - dh_i, 0, False)

    def ring(values, axis):
        count = lax.axis_size(axis)
        moved = [values]
        for k in range(1, count):
            moved.append(lax.ppermute(values, axis, [(i, (i - k) % count) for i in range(count)]))
        return moved

    inputs = tokens.reshape(tokens_row, width).astype(jnp.float32)
    qkv_row = lax.all_gather(w_qkv.reshape(width, -1), "row", axis=0)
    factor_one = lax.rsqrt(col_total(inputs * inputs) / D + EPS_NORM)
    far_routes = lax.ppermute(routes, "dh", far_pairs())
    far_gates = lax.ppermute(route_gates, "dh", far_pairs())
    ids = jnp.concatenate(ring(block_ids, "col"), axis=0)
    normed_one = (inputs * factor_one[:, None] * gains[0][None, :]).astype(low)
    normed_one = after(normed_one, far_routes, far_gates, ids)
    terms = jnp.einsum(
        "stf,gfh->sgth",
        normed_one.reshape(seqs_row, LEN, width),
        qkv_row,
        preferred_element_type=jnp.float32,
    )
    terms = terms.astype(low).reshape(col_n * LEN, -1)
    packed = lax.psum_scatter(terms, "col", scatter_dimension=0, tiled=True)

    ids = lax.dynamic_index_in_dim(ids, (row_i * seqs_row + seq_i - col_i) % col_n, 0, False)

    ranks, gates = slot_ranks(routes, route_gates)
    far_ranks, far_gates = slot_ranks(far_routes, far_gates)
    offsets = (jnp.arange(share) * slots).astype(jnp.int32)

    def unit_grid(values):
        values = values.reshape(dh_n, dl_n, row_n, col_n, token_block)
        return jnp.roll(values, -row_i * tokens_row, axis=-1)

    def unit_slots(ranks):
        return unit_grid(ranks[:, None, :] - offsets[None, :, None])

    def near(values):
        values = lax.dynamic_index_in_dim(values, dh_i, 0, False)
        return lax.dynamic_index_in_dim(values, row_i, 1, False)

    def here(values):
        return lax.dynamic_index_in_dim(values, col_i, 1, False)

    def unit_gates(gates):
        return here(near(unit_grid(jnp.broadcast_to(gates[:, None, :], (E, share, token_block)))))

    all_ranks = unit_slots(ranks)
    unit_ranks = [near(all_ranks), near(unit_slots(far_ranks))]
    here_ranks = [here(values) for values in unit_ranks]
    here_gates = [unit_gates(gates), unit_gates(far_gates)]

    def dispatch(number, blocks):
        ranks = unit_ranks[number].reshape(dl_n * col_n, token_block)
        return pick_slots(ranks, slots, [[block] for block in blocks])[:, 0]

    def to_experts(values):
        return to_owners(values, ("dl", "col")).reshape(dl_n, col_n, slots, width)

    def hot(number, k):
        chosen = unit_ranks[number][:, :, None, k * tokens_row : (k + 1) * tokens_row]
        return (chosen == jnp.arange(slots, dtype=jnp.int32)[None, None, :, None]).astype(low)

    def token_sums(number, values, half=0):
        def partial(k):
            own = values.reshape(dl_n, col_n, -1, slots, width)[:, :, half]
            return jnp.einsum("dcst,dcsf->tf", hot(number, k), own, preferred_element_type=jnp.float32)

        total = None
        for k in range(1, row_n):
            part = partial(k)
            values = after(values, part)
            part = lax.ppermute(part, "row", [(i, (i + k) % row_n) for i in range(row_n)])
            total = part if total is None else total + part
        return partial(0) + total, values

    def here_hot(number):
        return here_ranks[number][:, None, :] == jnp.arange(slots, dtype=jnp.int32)[None, :, None]

    slot_gate = jnp.stack(
        [
            jnp.sum(jnp.where(here_hot(number), here_gates[number][:, None, :], 0.0), axis=-1)
            for number in range(2)
        ],
        axis=1,
    )

    start = (dh_i * dl_n + dl_i) * experts_dp
    experts_in = jnp.swapaxes(lax.dynamic_slice_in_dim(w_gate_up, start, experts_dp, 0), 1, 2)
    in_pieces, down_pieces, piece_pairs = [], [], []
    for k in range(grid_n):
        kr, kc = k // col_n, k % col_n
        target = (((row_i - kr) % row_n) * col_n + (col_i - kc) % col_n) // share
        in_pieces.append(lax.dynamic_index_in_dim(experts_in, target, 0, False))
        down_pieces.append(lax.dynamic_index_in_dim(w_down, start + target, 0, False))
        piece_pairs.append(
            [
                (r * col_n + c, ((r - kr) % row_n) * col_n + (c - kc) % col_n)
                for r in range(row_n)
                for c in range(col_n)
            ]
        )

    grad_rows = cotangent.reshape(tokens_row, width)
    grad_low = grad_rows.astype(low)
    far_low = to_owners(jnp.broadcast_to(grad_low, (dh_n,) + grad_low.shape), "dh")

    def dispatch_wide(number, blocks):
        return pick_slots(here_ranks[number], slots, blocks)

    def by_row(blocks):
        parts = [ring(block, "row") for block in blocks]
        return [[part[k] for part in parts] for k in range(row_n)]

    own_wide = ring(after(grad_low, factor_one), "col")
    own_wide[-1] = after(own_wide[-1], terms, slot_gate, *here_ranks, *unit_ranks)
    own_picked = dispatch_wide(0, by_row(own_wide))

    mixed, log_total, tops = attend_forward(packed, ids)
    own_grads = to_owners(after(own_picked, mixed, far_low), "dl")
    my_gate = to_owners(after(slot_gate, own_grads), "dl")
    my_gate = jnp.swapaxes(my_gate, 0, 1)[..., None]
    far_low = after(far_low, mixed)
    far_low = lax.dynamic_index_in_dim(far_low, dh_n - 1 - dh_i, 0, False)
    far_wide = ring(far_low, "col")
    heads = lax.all_gather(mixed, "col", axis=0)
    heads = after(heads, *in_pieces, *down_pieces).reshape(seqs_row, KVH, LEN, GROUP * HD)
    out_row = lax.all_gather(after(w_out[0], packed), "row", axis=0)
    attn = jnp.einsum("sgth,ghf->stf", heads, out_row, preferred_element_type=jnp.float32)
    hidden = inputs + attn.reshape(tokens_row, width)

    factor_two = lax.rsqrt(col_total(hidden * hidden) / D + EPS_NORM)
    normed_two = (hidden * factor_two[:, None] * gains[1][None, :]).astype(low)
    normed_two = after(normed_two, far_wide[-1])
    far_two = from_far(normed_two)
    def spread(piece, pairs):
        return lax.ppermute(after(piece, normed_two), ("row", "col"), pairs)

    for k in range(1, grid_n):
        down_pieces[k] = spread(down_pieces[k], piece_pairs[k])
        in_pieces[k] = spread(in_pieces[k], piece_pairs[k])
    far_wide[-1] = after(far_wide[-1], down_pieces[col_n])
    far_picked = dispatch_wide(1, by_row(far_wide))
    far_grads = to_owners(after(far_picked, my_gate), "dl")
    place = jnp.stack([row_i, col_i]).astype(jnp.int32)
    weights_in, weights_down = join_weights(in_pieces, down_pieces, place, row_n, col_n)
    far_two = after(far_two, weights_in)
    far_slots = after(dispatch(1, ring(far_two, "row")), far_grads)
    far_rows = to_experts(far_slots)
    own_two = ring(normed_two, "row")
    own_two[-1] = after(own_two[-1], far_slots)
    own_slots = dispatch(0, own_two)
    own_rows = to_experts(after(own_slots, far_rows))

    far_back, far_weighted, far_pair = expert_passes(
        place, far_rows, far_grads, my_gate[1], weights_in, weights_down
    )
    own_rows = after(own_rows, far_back)
    own_back, own_weighted, own_pair = expert_passes(
        place, own_rows, own_grads, my_gate[0], weights_in, weights_down
    )

    def send_back(values):
        return to_owners(values.reshape(dl_n * col_n, 1, slots, width), ("dl", "col"))

    far_back = send_back(far_back)
    slot_out = expert_outputs([own_weighted, far_weighted], weights_down)
    own_back = send_back(after(own_back, far_back))
    far_sums = token_sums(1, after(far_back, slot_out))[0].astype(low)
    in_grad, down_grad = expert_grads(
        place,
        [
            (own_rows, own_grads, after(own_weighted, far_sums), own_pair),
            (far_rows, far_grads, far_weighted, far_pair),
        ],
        row_n,
    )
    own_back = after(own_back, in_grad)
    far_sums = from_far(far_sums)
    slot_out = after(slot_out, own_back)
    slot_out = to_owners(slot_out.reshape((dl_n * col_n,) + slot_out.shape[2:]), ("dl", "col"))
    own_sums, _ = token_sums(0, own_back)
    grad_normed_two = own_sums + far_sums.astype(jnp.float32)

    def block_grads(grads):
        grads = to_owners(grads.reshape((grid_n,) + grads.shape[2:]), ("row", "col"))
        if share > 1:
            grads = grads.astype(jnp.float32)
            grads = jnp.sum(grads.reshape((experts_dp, share) + grads.shape[1:]), axis=1)
        return grads


    grad_hidden_norm, grad_gain_two = norm_backward(hidden, factor_two, gains[1], grad_normed_two)
    grad_hidden = grad_rows + grad_hidden_norm
    grad_attn = grad_hidden.astype(low)
    terms = jnp.einsum(
        "stf,ghf->sgth",
        grad_attn.reshape(seqs_row, LEN, width),
        out_row,
        preferred_element_type=jnp.float32,
    )
    terms = terms.astype(low).reshape(col_n * LEN, -1)
    grad_heads = lax.psum_scatter(terms, "col", scatter_dimension=0, tiled=True)
    full_top = jnp.full((KVH, GROUP), -1e30, jnp.float32)
    full_top = lax.dynamic_update_slice(
        full_top, jnp.max(tops, axis=(1, 2))[None], (group_i, jnp.zeros((), jnp.int32))
    )
    far_out_sums, slot_out = token_sums(1, after(slot_out, terms), 1)
    far_out_sums = far_out_sums.astype(low)
    grad_heads = after(grad_heads, far_out_sums)
    far_out_sums = to_owners(jnp.broadcast_to(far_out_sums, (dh_n,) + far_out_sums.shape), "dh")
    grad_packed = attend_backward(packed, ids, log_total, grad_heads)
    packed_all = lax.all_gather(grad_packed, "col", axis=0).reshape(seqs_row, KVH, LEN, -1)

    own_out_sums, _ = token_sums(0, after(slot_out, grad_packed))
    packed_all = after(packed_all, own_out_sums)
    grad_down = block_grads(after(down_grad, far_out_sums))

    def owner_sums(left, right):
        columns = right.shape[-1]

        def term(k):
            group = lax.dynamic_index_in_dim(right, (row_i + k) % row_n, 1, False)
            return jnp.einsum("stf,sth->fh", left, group, preferred_element_type=jnp.float32)

        total = None
        for k in range(1, row_n):
            part = term(k)
            left = after(left, part)
            part = lax.ppermute(part, "row", [(i, (i + k) % row_n) for i in range(row_n)])
            total = part if total is None else total + part
        return (term(0) + total).astype(low)

    def dp_sums(total):
        parts = to_owners(total, ("dh", "dl")).reshape(dp_n, -1, total.shape[1])
        return jnp.sum(parts.astype(jnp.float32), axis=0)

    grad_normed_one = jnp.einsum(
        "sgth,gfh->stf", packed_all, qkv_row, preferred_element_type=jnp.float32
    ).reshape(tokens_row, width)
    out_total = owner_sums(grad_attn.reshape(seqs_row, LEN, width), after(heads, grad_heads))
    grad_gate_up = jnp.swapaxes(block_grads(after(in_grad, packed_all)), 1, 2)
    grad_gate_up = with_layout_constraint(grad_gate_up, Layout((0, 1, 2, 3)))
    qkv_total = owner_sums(normed_one.reshape(seqs_row, LEN, width), packed_all)
    far_out_sums = after(far_out_sums, qkv_total)
    far_out_sums = lax.dynamic_index_in_dim(far_out_sums, dh_n - 1 - dh_i, 0, False)
    block_output = hidden + own_out_sums + far_out_sums.astype(jnp.float32)
    totals = after(jnp.concatenate([qkv_total, out_total], axis=1), grad_gate_up)
    grad_gate_up, grad_down = after(grad_gate_up, qkv_total), after(grad_down, qkv_total)
    totals = dp_sums(totals)
    grad_qkv, grad_out = totals[:, None, : qkv_total.shape[1]], totals[:, qkv_total.shape[1] :].T[None]
    grad_normed_one = after(grad_normed_one, qkv_total)
    grad_input_norm, grad_gain_one = norm_backward(inputs, factor_one, gains[0], grad_normed_one)
    input_grad = grad_hidden + grad_input_norm

    full_top = butterfly(after(full_top, packed_all), jnp.maximum, ("col",))

    tops_row = jnp.pad(full_top.reshape(1, -1), ((0, 0), (0, width - KVH * GROUP)))
    small = jnp.concatenate([grad_gain_one[None], grad_gain_two[None], tops_row])

    def combine(left, right):
        return jnp.concatenate([left[:2] + right[:2], jnp.maximum(left[2:], right[2:])])

    small = butterfly(small, combine, ("row", "dh", "dl"))
    grad_gains, head_top = small[:2], small[2, : KVH * GROUP].reshape(KVH, GROUP)

    factors = TAU_CLIP / jnp.maximum(head_top, TAU_CLIP)
    local_factors = lax.dynamic_slice_in_dim(factors, row_i, 1, 0)
    query_scale = jnp.repeat(jnp.sqrt(local_factors), HD, axis=1)
    key_scale = jnp.repeat(jnp.sqrt(jnp.min(local_factors, axis=1, keepdims=True)), HD, axis=1)
    column_scale = jnp.concatenate([query_scale, key_scale, jnp.ones_like(key_scale)], axis=1)
    qkv_new, qkv_one, qkv_two = adam_step(
        qkv_master, qkv_first, qkv_second, grad_qkv, D ** (-0.5), DECAY_RATE
    )
    qkv_new = qkv_new * column_scale[None]
    out_new, out_one, out_two = adam_step(
        out_master, out_first, out_second, grad_out, max(D // 192, 1) ** (-0.5), DECAY_RATE
    )
    gate_up_new, gate_up_one, gate_up_two = adam_step(
        gate_up_master, gate_up_first, gate_up_second, grad_gate_up, D ** (-0.5), DECAY_RATE
    )
    down_new, down_one, down_two = adam_step(
        down_master, down_first, down_second, grad_down, FFE ** (-0.5), DECAY_RATE
    )
    gains_new, gains_one, gains_two = adam_step(
        gains, gain_first, gain_second, grad_gains, 0.2, 0.0
    )
    return (
        block_output.reshape(1, -1, 2 * width),
        input_grad.reshape(1, -1, 2 * width),
        qkv_new,
        qkv_one,
        qkv_two,
        qkv_new.astype(jnp.bfloat16),
        out_new,
        out_one,
        out_two,
        out_new.astype(jnp.bfloat16),
        gate_up_new,
        gate_up_one,
        gate_up_two,
        gate_up_new.astype(jnp.bfloat16),
        down_new,
        down_one,
        down_two,
        down_new.astype(jnp.bfloat16),
        gains_new,
        gains_one,
        gains_two,
        factors.reshape(-1),
    )


def solution(mesh):
    devices = mesh.devices
    devices = devices.reshape((2, devices.shape[0] // 2) + devices.shape[1:])
    mesh = jax.sharding.Mesh(devices, ("dh", "dl", "row", "col"))
    dp = ("dh", "dl")
    in_specs = (
        P("col", (*dp, "row"), None),
        P("col", (*dp, "row"), None),
        P(None, dp),
        P(None, dp),
        P((*dp, "col"), None),
        P("col", "row", None),
        P("row", None, "col"),
        P(None, "col", None, "row"),
        P(None, "row", "col"),
        P(None, "col"),
        P(None, "col"),
        P(None, "col"),
        P(("col", *dp), "row", None),
        P(("col", *dp), "row", None),
        P(("col", *dp), "row", None),
        P("row", None, ("col", *dp)),
        P("row", None, ("col", *dp)),
        P("row", None, ("col", *dp)),
        P(dp, "col", None, "row"),
        P(dp, "col", None, "row"),
        P(dp, "col", None, "row"),
        P(dp, "row", "col"),
        P(dp, "row", "col"),
        P(dp, "row", "col"),
    )
    out_specs = (
        P("col", (*dp, "row"), None),
        P("col", (*dp, "row"), None),
        P(("col", *dp), "row", None),
        P(("col", *dp), "row", None),
        P(("col", *dp), "row", None),
        P(("col", *dp), "row", None),
        P("row", None, ("col", *dp)),
        P("row", None, ("col", *dp)),
        P("row", None, ("col", *dp)),
        P("row", None, ("col", *dp)),
        P(dp, "col", None, "row"),
        P(dp, "col", None, "row"),
        P(dp, "col", None, "row"),
        P(dp, "col", None, "row"),
        P(dp, "row", "col"),
        P(dp, "row", "col"),
        P(dp, "row", "col"),
        P(dp, "row", "col"),
        P(None, "col"),
        P(None, "col"),
        P(None, "col"),
        P(),
    )
    return jax.shard_map(
        on_device, mesh=mesh, in_specs=in_specs, out_specs=out_specs, check_vma=False
    )
```

```python
import functools

import jax
import jax.numpy as jnp
from jax import lax
from jax.experimental import pallas as pl
from jax.experimental.layout import Layout, with_layout_constraint
from jax.experimental.pallas import tpu as pltpu
from jax.sharding import PartitionSpec as P

D = 1536
KVH = 2
HD = 128
E = 32
FFE = 768
TOP = 4
GROUP = 6
LEN = 1024
STEP = 5


EPS_NORM = 1e-06
BETA_ONE = 0.5
BETA_TWO = 0.5
ADAM_EPS = 1e-08
DECAY_RATE = 0.1
TAU_CLIP = 3.0


QUERIES = 256
MIB = 1 << 20
NO_COST = pl.CostEstimate(flops=0, bytes_accessed=0, transcendentals=0)
LONG = pl.CostEstimate(flops=10**11, bytes_accessed=0, transcendentals=0)


def dot(left, right, left_dim=1, right_dim=0):
    return lax.dot_general(
        left, right, (((left_dim,), (right_dim,)), ((), ())), preferred_element_type=jnp.float32
    )


def pass_on(*refs):
    pass


def after(values, *earlier):
    return pl.pallas_call(
        pass_on,
        in_specs=[pl.BlockSpec(memory_space=pl.ANY)] * (1 + len(earlier)),
        out_specs=pl.BlockSpec(memory_space=pl.ANY),
        out_shape=jax.ShapeDtypeStruct(values.shape, values.dtype),
        input_output_aliases={0: 0},
        cost_estimate=NO_COST,
    )(values, *earlier)


def col_total(values):
    return lax.psum(jnp.sum(values, axis=1), "col")


def butterfly(values, combine, axes):
    for axis in axes:
        count = lax.axis_size(axis)
        bit = 1
        while bit < count:
            pairs = [(i, i ^ bit) for i in range(count)]
            values = combine(values, lax.ppermute(values, axis, pairs))
            bit *= 2
    return values


def norm_backward(values, factor, gain, grad_normed):
    inner = col_total(values * gain[None, :] * grad_normed) / D
    grad_values = (
        factor[:, None] * gain[None, :] * grad_normed - values * (factor**3 * inner)[:, None]
    )
    grad_gain = jnp.sum(grad_normed * values * factor[:, None], axis=0)
    return (grad_values, grad_gain)


def to_owners(values, axes):
    return lax.all_to_all(values, axes, split_axis=0, concat_axis=0, tiled=True)


def slot_ranks(routes, route_gates):
    tokens = routes.shape[1]
    hits = routes[:, None, :] == jnp.arange(E, dtype=jnp.int32)[None, :, None]
    gates = jnp.sum(jnp.where(hits, route_gates[:, None, :], 0.0), axis=0)
    chosen = jnp.any(hits, axis=0)
    lanes = jnp.arange(128)
    upto = (lanes[:, None] <= lanes[None, :]).astype(jnp.bfloat16)
    runs = jnp.einsum(
        "ebt,ts->ebs",
        chosen.reshape(E, tokens // 128, 128).astype(jnp.bfloat16),
        upto,
        preferred_element_type=jnp.float32,
    ).astype(jnp.int32)
    totals = runs[:, :, -1]
    ranks = (runs + (jnp.cumsum(totals, axis=1) - totals)[:, :, None]).reshape(E, tokens) - 1
    return (jnp.where(chosen, ranks, -1), gates)


def key_reach(chunk):
    return min((chunk + 2) * QUERIES, LEN)


def scores_turned(queries, keys, id_row, id_col):
    scores = dot(keys, queries, 1, 1) * HD ** (-0.5)
    return jnp.where(id_col <= id_row, scores, -1e30)


def attend_kernel(query_ref, key_ref, value_ref, id_row_ref, id_col_ref, mixed_ref, log_ref, top_ref):
    value_turned = value_ref[...].T
    for chunk in range(LEN // QUERIES):
        rows = slice(chunk * QUERIES, (chunk + 1) * QUERIES)
        reach = key_reach(chunk)
        masked = scores_turned(
            query_ref[rows, :], key_ref[:reach, :], id_row_ref[:, rows], id_col_ref[:reach, :]
        )
        top = jnp.max(masked, axis=0, keepdims=True)
        weights = jnp.exp(masked - top)
        total = jnp.sum(weights, axis=0, keepdims=True)
        probs = (weights * (1.0 / total)).astype(jnp.bfloat16)
        mixed_ref[rows, :] = dot(value_turned[:, :reach], probs).T.astype(jnp.bfloat16)
        log_ref[0, :, rows] = top + jnp.log(total)
        top_ref[0, :, rows] = top


def attend_forward(packed, blocks):
    head = pl.BlockSpec((LEN, HD), lambda h: (0, h))
    row = pl.BlockSpec((1, 1, LEN), lambda h: (h, 0, 0))
    return pl.pallas_call(
        attend_kernel,
        grid=(GROUP,),
        in_specs=[
            head,
            pl.BlockSpec((LEN, HD), lambda h: (0, GROUP)),
            pl.BlockSpec((LEN, HD), lambda h: (0, GROUP + 1)),
            pl.BlockSpec((1, LEN), lambda h: (0, 0)),
            pl.BlockSpec((LEN, 1), lambda h: (0, 0)),
        ],
        out_specs=[head, row, row],
        out_shape=[
            jax.ShapeDtypeStruct((LEN, GROUP * HD), jnp.bfloat16),
            jax.ShapeDtypeStruct((GROUP, 1, LEN), jnp.float32),
            jax.ShapeDtypeStruct((GROUP, 1, LEN), jnp.float32),
        ],
        compiler_params=pltpu.CompilerParams(vmem_limit_bytes=40 * MIB),
        cost_estimate=NO_COST,
    )(packed, packed, packed, blocks[None, :], blocks[:, None])


def attend_back_kernel(
    query_ref, key_ref, value_ref, grad_ref, log_ref, id_row_ref, id_col_ref, out_ref, keys_acc, values_acc
):
    head = pl.program_id(0)

    @pl.when(head == 0)
    def _():
        keys_acc[...] = jnp.zeros_like(keys_acc)
        values_acc[...] = jnp.zeros_like(values_acc)

    key_turned = key_ref[...].T
    for chunk in range(LEN // QUERIES):
        rows = slice(chunk * QUERIES, (chunk + 1) * QUERIES)
        reach = key_reach(chunk)
        queries = query_ref[rows, :]
        grads = grad_ref[rows, :]
        masked = scores_turned(queries, key_ref[:reach, :], id_row_ref[:, rows], id_col_ref[:reach, :])
        probs = jnp.exp(masked - log_ref[0, :, rows])
        grad_probs = dot(value_ref[:reach, :], grads, 1, 1)
        delta = jnp.sum(probs * grad_probs, axis=0, keepdims=True)
        grad_scores = (probs * (grad_probs - delta)).astype(jnp.bfloat16)
        values_acc[:reach, :] += dot(probs.astype(jnp.bfloat16), grads)
        keys_acc[:reach, :] += dot(grad_scores, queries)
        grad_query = dot(key_turned[:, :reach], grad_scores).T * HD ** (-0.5)
        lanes = pl.ds(pl.multiple_of(head * HD, HD), HD)
        out_ref[rows, lanes] = grad_query.astype(jnp.bfloat16)

    @pl.when(head == GROUP - 1)
    def _():
        out_ref[:, GROUP * HD : (GROUP + 1) * HD] = (keys_acc[...] * HD ** (-0.5)).astype(jnp.bfloat16)
        out_ref[:, (GROUP + 1) * HD :] = values_acc[...].astype(jnp.bfloat16)


def attend_backward(packed, blocks, log_total, grad_heads):
    head = pl.BlockSpec((LEN, HD), lambda h: (0, h))
    return pl.pallas_call(
        attend_back_kernel,
        grid=(GROUP,),
        in_specs=[
            head,
            pl.BlockSpec((LEN, HD), lambda h: (0, GROUP)),
            pl.BlockSpec((LEN, HD), lambda h: (0, GROUP + 1)),
            head,
            pl.BlockSpec((1, 1, LEN), lambda h: (h, 0, 0)),
            pl.BlockSpec((1, LEN), lambda h: (0, 0)),
            pl.BlockSpec((LEN, 1), lambda h: (0, 0)),
        ],
        out_specs=pl.BlockSpec((LEN, (GROUP + 2) * HD), lambda h: (0, 0)),
        out_shape=jax.ShapeDtypeStruct((LEN, (GROUP + 2) * HD), jnp.bfloat16),
        scratch_shapes=[pltpu.VMEM((LEN, HD), jnp.float32)] * 2,
        compiler_params=pltpu.CompilerParams(vmem_limit_bytes=40 * MIB),
        cost_estimate=NO_COST,
    )(packed, packed, packed, grad_heads, log_total, blocks[None, :], blocks[:, None])


def pick_kernel(ranks_ref, *refs):
    blocks, out_ref = refs[:-1], refs[-1]
    _, cols, slots, _ = out_ref.shape
    rows = len(blocks) // cols
    count = blocks[0].shape[0]
    slot = lax.broadcasted_iota(jnp.int32, (slots, rows * count), 0)
    hot = (ranks_ref[0] == slot).astype(jnp.float32).astype(jnp.bfloat16)
    for c in range(cols):
        picked = dot(hot[:, :count], blocks[c][...])
        for k in range(1, rows):
            picked += dot(hot[:, k * count : (k + 1) * count], blocks[k * cols + c][...])
        out_ref[0, c] = picked.astype(jnp.bfloat16)


def pick_slots(ranks, slots, blocks, cost=NO_COST):
    units, count = ranks.shape
    cols = len(blocks[0])
    flat = [block for row in blocks for block in row]
    width = flat[0].shape[1]
    whole = pl.BlockSpec(flat[0].shape, lambda u: (0, 0), pipeline_mode=pl.Buffered(1))
    return pl.pallas_call(
        pick_kernel,
        grid=(units,),
        in_specs=[pl.BlockSpec((1, 1, count), lambda u: (u, 0, 0))] + [whole] * len(flat),
        out_specs=pl.BlockSpec((1, cols, slots, width), lambda u: (u, 0, 0, 0)),
        out_shape=jax.ShapeDtypeStruct((units, cols, slots, width), jnp.bfloat16),
        compiler_params=pltpu.CompilerParams(vmem_limit_bytes=56 * MIB),
        cost_estimate=cost,
    )(ranks[:, None, :], *flat)


def expert_kernel(col_n, place_ref, rows_ref, grads_ref, gate_ref, in_ref, down_ref, back_ref, weighted_ref, pair_ref):
    gate_up = dot(rows_ref[0, 0], in_ref[0])
    grad_weighted = dot(grads_ref[0, 0], down_ref[place_ref[1]], 1, 1)
    for c in range(1, col_n):
        gate_up += dot(rows_ref[0, c], in_ref[c])
        grad_weighted += dot(grads_ref[0, c], down_ref[lax.rem(place_ref[1] + c, col_n)], 1, 1)
    gate_half, up_half, scale = gate_up[:, :FFE], gate_up[:, FFE:], gate_ref[0]
    sigmoid_gate = jax.nn.sigmoid(gate_half)
    silu_gate = gate_half * sigmoid_gate
    weighted_ref[0] = (silu_gate * up_half * scale).astype(jnp.bfloat16)
    grad_act = grad_weighted * scale
    grad_gate = grad_act * up_half * sigmoid_gate * (1.0 + gate_half * (1.0 - sigmoid_gate))
    pair_ref[0, :, :FFE] = grad_gate.astype(jnp.bfloat16)
    pair_ref[0, :, FFE:] = (grad_act * silu_gate).astype(jnp.bfloat16)
    for c in range(col_n):
        back_ref[0, c] = dot(pair_ref[0], in_ref[c], 1, 1).astype(jnp.bfloat16)


def expert_passes(place, slot_rows, slot_grads, gates, weights_in, weights_down):
    dl_n, col_n, slots, width = slot_rows.shape
    block = pl.BlockSpec((1, col_n, slots, width), lambda d: (d, 0, 0, 0))
    return pl.pallas_call(
        functools.partial(expert_kernel, col_n),
        grid=(dl_n,),
        in_specs=[
            pl.BlockSpec(memory_space=pltpu.SMEM),
            block,
            block,
            pl.BlockSpec((1, slots, 1), lambda d: (d, 0, 0)),
            pl.BlockSpec(weights_in.shape, lambda d: (0, 0, 0)),
            pl.BlockSpec(weights_down.shape, lambda d: (0, 0, 0)),
        ],
        out_specs=[
            block,
            pl.BlockSpec((1, slots, FFE), lambda d: (d, 0, 0)),
            pl.BlockSpec((1, slots, 2 * FFE), lambda d: (d, 0, 0)),
        ],
        out_shape=[
            jax.ShapeDtypeStruct(slot_rows.shape, jnp.bfloat16),
            jax.ShapeDtypeStruct((dl_n, slots, FFE), jnp.bfloat16),
            jax.ShapeDtypeStruct((dl_n, slots, 2 * FFE), jnp.bfloat16),
        ],
        compiler_params=pltpu.CompilerParams(vmem_limit_bytes=56 * MIB),
        cost_estimate=NO_COST,
    )(place, slot_rows, slot_grads, gates, weights_in, weights_down)


def join_kernel(row_n, col_n, place_ref, *refs):
    count = row_n * col_n
    in_refs, down_refs, (in_out, down_out) = refs[:count], refs[count : 2 * count], refs[2 * count :]
    part = FFE // row_n
    for k in range(count):
        r = lax.rem(place_ref[0] + k // col_n, row_n)
        c = lax.rem(place_ref[1] + k % col_n, col_n)
        for g in range(2):
            lanes = pl.ds(pl.multiple_of(g * FFE + r * part, 128), part)
            in_out[c, :, lanes] = in_refs[k][g]
        down_out[c, pl.ds(pl.multiple_of(r * part, 128), part), :] = down_refs[k][...]


def join_weights(in_pieces, down_pieces, place, row_n, col_n):
    width = in_pieces[0].shape[1]
    return pl.pallas_call(
        functools.partial(join_kernel, row_n, col_n),
        in_specs=[pl.BlockSpec(memory_space=pltpu.SMEM)]
        + [pl.BlockSpec(memory_space=pltpu.VMEM)] * (2 * row_n * col_n),
        out_specs=[pl.BlockSpec(memory_space=pltpu.VMEM)] * 2,
        out_shape=[
            jax.ShapeDtypeStruct((col_n, width, 2 * FFE), jnp.bfloat16),
            jax.ShapeDtypeStruct((col_n, FFE, width), jnp.bfloat16),
        ],
        compiler_params=pltpu.CompilerParams(vmem_limit_bytes=40 * MIB),
        cost_estimate=NO_COST,
    )(place, *in_pieces, *down_pieces)


def halves(steps, sets):
    return [lambda d, number=number: jnp.clip(d - number * steps, 0, steps - 1) for number in range(sets)]


def expert_out_kernel(sets, steps, down_ref, *refs):
    out_ref = refs[sets]
    for number in range(sets):

        @pl.when(pl.program_id(0) // steps == number)
        def _():
            blocks, slots, _ = refs[number].shape
            weighted = refs[number][...].reshape(blocks * slots, FFE)
            for c in range(down_ref.shape[0]):
                slot_out = dot(weighted, down_ref[c]).astype(jnp.bfloat16)
                out_ref[:, c, 0] = slot_out.reshape(blocks, slots, -1)


def expert_outputs(weighted, weights_down):
    dl_n, slots, _ = weighted[0].shape
    col_n, _, width = weights_down.shape
    sets = len(weighted)
    blocks = 2 if dl_n % 2 == 0 else 1
    steps = dl_n // blocks
    return pl.pallas_call(
        functools.partial(expert_out_kernel, sets, steps),
        grid=(sets * steps,),
        in_specs=[pl.BlockSpec(weights_down.shape, lambda d: (0, 0, 0))]
        + [
            pl.BlockSpec((blocks, slots, FFE), lambda d, at=at: (at(d), 0, 0)) for at in halves(steps, sets)
        ],
        out_specs=pl.BlockSpec(
            (blocks, col_n, 1, slots, width), lambda d: (lax.rem(d, steps), 0, d // steps, 0, 0)
        ),
        out_shape=jax.ShapeDtypeStruct((dl_n, col_n, sets, slots, width), jnp.bfloat16),
        compiler_params=pltpu.CompilerParams(vmem_limit_bytes=40 * MIB),
        cost_estimate=NO_COST,
    )(weights_down, *weighted)


def expert_grad_kernel(row_n, sets, steps, place_ref, *refs):
    part = FFE // row_n
    step = pl.program_id(1)
    in_grad_ref, down_grad_ref, in_acc, down_acc = refs[4 * sets :]

    @pl.when(step == 0)
    def _():
        in_acc[...] = jnp.zeros_like(in_acc)
        down_acc[...] = jnp.zeros_like(down_acc)

    for number in range(sets):
        rows_ref, grads_ref, weighted_ref, pair_ref = refs[4 * number : 4 * number + 4]

        @pl.when(step // steps == number)
        def _():
            blocks, _, slots, width = rows_ref.shape
            weighted = weighted_ref[...].reshape(blocks * slots, FFE)
            pair = pair_ref[...].reshape(blocks * slots, 2 * FFE)
            rows = rows_ref[...].reshape(blocks * slots, width)
            grads = grads_ref[...].reshape(blocks * slots, width)
            in_acc[...] += dot(rows, pair, 0, 0)
            down_acc[...] += dot(weighted, grads, 0, 0)

    @pl.when(step == sets * steps - 1)
    def _():
        for r in range(row_n):
            for g in range(2):
                lanes = slice(g * FFE + r * part, g * FFE + (r + 1) * part)
                in_grad_ref[r, 0, g] = in_acc[:, lanes].astype(jnp.bfloat16)
            down_grad_ref[r, 0] = down_acc[r * part : (r + 1) * part, :].astype(jnp.bfloat16)


def expert_grads(place, sources, row_n):
    dl_n, col_n, slots, width = sources[0][0].shape
    sets = len(sources)
    blocks = 2 if dl_n % 2 == 0 else 1
    steps = dl_n // blocks
    part = FFE // row_n
    in_specs = []
    for at in halves(steps, sets):
        in_specs += [
            pl.BlockSpec((blocks, 1, slots, width), lambda c, d, p, at=at: (at(d), c, 0, 0)),
            pl.BlockSpec(
                (blocks, 1, slots, width),
                lambda c, d, p, at=at: (at(d), lax.rem(c - p[1] + col_n, col_n), 0, 0),
            ),
            pl.BlockSpec((blocks, slots, FFE), lambda c, d, p, at=at: (at(d), 0, 0)),
            pl.BlockSpec((blocks, slots, 2 * FFE), lambda c, d, p, at=at: (at(d), 0, 0)),
        ]
    return pl.pallas_call(
        functools.partial(expert_grad_kernel, row_n, sets, steps),
        grid_spec=pltpu.PrefetchScalarGridSpec(
            num_scalar_prefetch=1,
            grid=(col_n, sets * steps),
            in_specs=in_specs,
            out_specs=[
                pl.BlockSpec((row_n, 1, 2, width, part), lambda c, d, p: (0, c, 0, 0, 0)),
                pl.BlockSpec((row_n, 1, part, width), lambda c, d, p: (0, c, 0, 0)),
            ],
            scratch_shapes=[
                pltpu.VMEM((width, 2 * FFE), jnp.float32),
                pltpu.VMEM((FFE, width), jnp.float32),
            ],
        ),
        out_shape=[
            jax.ShapeDtypeStruct((row_n, col_n, 2, width, part), jnp.bfloat16),
            jax.ShapeDtypeStruct((row_n, col_n, part, width), jnp.bfloat16),
        ],
        compiler_params=pltpu.CompilerParams(vmem_limit_bytes=58 * MIB),
        cost_estimate=LONG,
    )(place, *[array for source in sources for array in source])


def adam_step(master, moment_one, moment_two, gradient, rate, decay):
    first = BETA_ONE * moment_one + (1.0 - BETA_ONE) * gradient
    second = BETA_TWO * moment_two + (1.0 - BETA_TWO) * gradient * gradient
    first_hat = first / (1.0 - BETA_ONE**STEP)
    second_hat = second / (1.0 - BETA_TWO**STEP)
    updated = master - rate * (first_hat / (jnp.sqrt(second_hat) + ADAM_EPS) + decay * master)
    return (updated, first, second)


def on_device(
    tokens,
    cotangent,
    routes,
    route_gates,
    block_ids,
    w_qkv,
    w_out,
    w_gate_up,
    w_down,
    gains,
    gain_first,
    gain_second,
    qkv_master,
    qkv_first,
    qkv_second,
    out_master,
    out_first,
    out_second,
    gate_up_master,
    gate_up_first,
    gate_up_second,
    down_master,
    down_first,
    down_second,
):
    dh_n, dl_n, row_n, col_n = (lax.axis_size(name) for name in ("dh", "dl", "row", "col"))
    dh_i, dl_i, row_i, col_i = (lax.axis_index(name) for name in ("dh", "dl", "row", "col"))
    dp_n = dh_n * dl_n
    grid_n = row_n * col_n
    width = w_qkv.shape[0]
    token_block = routes.shape[1]
    capacity = 5 * token_block * TOP // (4 * E)
    tokens_row = token_block // row_n
    seqs_row = tokens_row // LEN
    assert seqs_row * KVH == col_n and KVH == row_n
    seq_i, group_i = col_i // KVH, col_i % KVH
    experts_dp = E // dp_n
    share = grid_n // experts_dp
    assert share * experts_dp == grid_n
    slots = capacity // share
    low = jnp.bfloat16

    def far_pairs():
        return [(i, dh_n - 1 - i) for i in range(dh_n)]

    def from_far(values):
        both = lax.all_gather(values, "dh", axis=0)
        return lax.dynamic_index_in_dim(both, dh_n - 1 - dh_i, 0, False)

    def ring(values, axis):
        count = lax.axis_size(axis)
        moved = [values]
        for k in range(1, count):
            moved.append(lax.ppermute(values, axis, [(i, (i - k) % count) for i in range(count)]))
        return moved

    inputs = tokens.reshape(tokens_row, width).astype(jnp.float32)
    qkv_row = lax.all_gather(w_qkv.reshape(width, -1), "row", axis=0)
    factor_one = lax.rsqrt(col_total(inputs * inputs) / D + EPS_NORM)
    far_routes = lax.ppermute(routes, "dh", far_pairs())
    far_gates = lax.ppermute(route_gates, "dh", far_pairs())
    ids = jnp.concatenate(ring(block_ids, "col"), axis=0)
    normed_one = (inputs * factor_one[:, None] * gains[0][None, :]).astype(low)
    normed_one = after(normed_one, far_routes, far_gates, ids)
    terms = jnp.einsum(
        "stf,gfh->sgth",
        normed_one.reshape(seqs_row, LEN, width),
        qkv_row,
        preferred_element_type=jnp.float32,
    )
    terms = terms.astype(low).reshape(col_n * LEN, -1)
    packed = lax.psum_scatter(terms, "col", scatter_dimension=0, tiled=True)

    ids = lax.dynamic_index_in_dim(ids, (row_i * seqs_row + seq_i - col_i) % col_n, 0, False)

    ranks, gates = slot_ranks(routes, route_gates)
    far_ranks, far_gates = slot_ranks(far_routes, far_gates)
    offsets = (jnp.arange(share) * slots).astype(jnp.int32)

    def unit_grid(values):
        values = values.reshape(dh_n, dl_n, row_n, col_n, token_block)
        return jnp.roll(values, -row_i * tokens_row, axis=-1)

    def unit_slots(ranks):
        return unit_grid(ranks[:, None, :] - offsets[None, :, None])

    def near(values):
        values = lax.dynamic_index_in_dim(values, dh_i, 0, False)
        return lax.dynamic_index_in_dim(values, row_i, 1, False)

    def here(values):
        return lax.dynamic_index_in_dim(values, col_i, 1, False)

    def unit_gates(gates):
        return here(near(unit_grid(jnp.broadcast_to(gates[:, None, :], (E, share, token_block)))))

    all_ranks = unit_slots(ranks)
    unit_ranks = [near(all_ranks), near(unit_slots(far_ranks))]
    here_ranks = [here(values) for values in unit_ranks]
    here_gates = [unit_gates(gates), unit_gates(far_gates)]

    def dispatch(number, blocks):
        ranks = unit_ranks[number].reshape(dl_n * col_n, token_block)
        return pick_slots(ranks, slots, [[block] for block in blocks])[:, 0]

    def to_experts(values):
        return to_owners(values, ("dl", "col")).reshape(dl_n, col_n, slots, width)

    def hot(number, k):
        chosen = unit_ranks[number][:, :, None, k * tokens_row : (k + 1) * tokens_row]
        return (chosen == jnp.arange(slots, dtype=jnp.int32)[None, None, :, None]).astype(low)

    def to_row(part, k, pieces):
        pairs = [(i, (i + k) % row_n) for i in range(row_n)]
        return jnp.concatenate([lax.ppermute(piece, "row", pairs) for piece in jnp.split(part, pieces)])

    def token_sums(number, values, half=0, pieces=1):
        def partial(k):
            own = values.reshape(dl_n, col_n, -1, slots, width)[:, :, half]
            return jnp.einsum("dcst,dcsf->tf", hot(number, k), own, preferred_element_type=jnp.float32)

        total = None
        for k in range(1, row_n):
            part = partial(k)
            values = after(values, part)
            part = to_row(part, k, pieces)
            total = part if total is None else total + part
        return partial(0) + total, values

    def here_hot(number):
        return here_ranks[number][:, None, :] == jnp.arange(slots, dtype=jnp.int32)[None, :, None]

    slot_gate = jnp.stack(
        [
            jnp.sum(jnp.where(here_hot(number), here_gates[number][:, None, :], 0.0), axis=-1)
            for number in range(2)
        ],
        axis=1,
    )

    start = (dh_i * dl_n + dl_i) * experts_dp
    experts_in = jnp.swapaxes(lax.dynamic_slice_in_dim(w_gate_up, start, experts_dp, 0), 1, 2)
    in_pieces, down_pieces, piece_pairs = [], [], []
    for k in range(grid_n):
        kr, kc = k // col_n, k % col_n
        target = (((row_i - kr) % row_n) * col_n + (col_i - kc) % col_n) // share
        in_pieces.append(lax.dynamic_index_in_dim(experts_in, target, 0, False))
        down_pieces.append(lax.dynamic_index_in_dim(w_down, start + target, 0, False))
        piece_pairs.append(
            [
                (r * col_n + c, ((r - kr) % row_n) * col_n + (c - kc) % col_n)
                for r in range(row_n)
                for c in range(col_n)
            ]
        )

    grad_rows = cotangent.reshape(tokens_row, width)
    grad_low = grad_rows.astype(low)
    far_low = to_owners(jnp.broadcast_to(grad_low, (dh_n,) + grad_low.shape), "dh")

    def dispatch_wide(number, blocks, cost=NO_COST):
        return pick_slots(here_ranks[number], slots, blocks, cost)

    def by_row(blocks):
        parts = [ring(block, "row") for block in blocks]
        return [[part[k] for part in parts] for k in range(row_n)]

    own_wide = ring(after(grad_low, factor_one), "col")
    own_wide[-1] = after(own_wide[-1], terms, slot_gate, *here_ranks, *unit_ranks)
    own_picked = dispatch_wide(0, by_row(own_wide))

    mixed, log_total, tops = attend_forward(packed, ids)
    own_grads = to_owners(after(own_picked, mixed, far_low), "dl")
    my_gate = to_owners(after(slot_gate, own_grads), "dl")
    my_gate = jnp.swapaxes(my_gate, 0, 1)[..., None]
    far_low = after(far_low, mixed)
    far_low = lax.dynamic_index_in_dim(far_low, dh_n - 1 - dh_i, 0, False)
    far_wide = ring(far_low, "col")
    heads = lax.all_gather(mixed, "col", axis=0)
    out_row = jnp.roll(jnp.stack(ring(w_out[0], "row")), row_i, axis=0)
    heads = after(heads, out_row, *in_pieces, *down_pieces).reshape(seqs_row, KVH, LEN, GROUP * HD)
    attn = jnp.einsum("sgth,ghf->stf", heads, out_row, preferred_element_type=jnp.float32)
    hidden = inputs + attn.reshape(tokens_row, width)

    factor_two = lax.rsqrt(col_total(hidden * hidden) / D + EPS_NORM)
    normed_two = (hidden * factor_two[:, None] * gains[1][None, :]).astype(low)
    normed_two = after(normed_two, far_wide[-1])
    far_two = from_far(normed_two)
    def spread(piece, pairs):
        return lax.ppermute(after(piece, normed_two), ("row", "col"), pairs)

    for k in range(1, grid_n):
        down_pieces[k] = spread(down_pieces[k], piece_pairs[k])
        in_pieces[k] = spread(in_pieces[k], piece_pairs[k])
    far_wide[-1] = after(far_wide[-1], down_pieces[col_n])
    far_picked = dispatch_wide(1, by_row(far_wide), LONG)
    far_grads = to_owners(after(far_picked, my_gate), "dl")
    place = jnp.stack([row_i, col_i]).astype(jnp.int32)
    weights_in, weights_down = join_weights(in_pieces, down_pieces, place, row_n, col_n)
    far_two = after(far_two, weights_in)
    far_slots = after(dispatch(1, ring(far_two, "row")), far_grads)
    far_rows = to_experts(far_slots)
    own_two = ring(normed_two, "row")
    own_two[-1] = after(own_two[-1], far_slots)
    own_slots = dispatch(0, own_two)
    own_rows = to_experts(after(own_slots, far_rows))

    far_back, far_weighted, far_pair = expert_passes(
        place, far_rows, far_grads, my_gate[1], weights_in, weights_down
    )
    own_rows = after(own_rows, far_back)
    own_back, own_weighted, own_pair = expert_passes(
        place, own_rows, own_grads, my_gate[0], weights_in, weights_down
    )

    def send_back(values):
        return to_owners(values.reshape(dl_n * col_n, 1, slots, width), ("dl", "col"))

    far_back = send_back(far_back)
    slot_out = expert_outputs([own_weighted, far_weighted], weights_down)
    own_back = send_back(after(own_back, far_back))
    far_sums = token_sums(1, after(far_back, slot_out))[0].astype(low)
    in_grad, down_grad = expert_grads(
        place,
        [
            (own_rows, own_grads, after(own_weighted, far_sums), own_pair),
            (far_rows, far_grads, far_weighted, far_pair),
        ],
        row_n,
    )
    own_back = after(own_back, in_grad)
    far_sums = lax.ppermute(far_sums, "dh", far_pairs())
    slot_out = after(slot_out, own_back)
    slot_out = to_owners(slot_out.reshape((dl_n * col_n,) + slot_out.shape[2:]), ("dl", "col"))
    own_sums, _ = token_sums(0, own_back, pieces=4)
    grad_normed_two = own_sums + far_sums.astype(jnp.float32)

    def block_grads(grads):
        grads = to_owners(grads.reshape((grid_n,) + grads.shape[2:]), ("row", "col"))
        if share > 1:
            grads = grads.astype(jnp.float32)
            grads = jnp.sum(grads.reshape((experts_dp, share) + grads.shape[1:]), axis=1)
        return grads


    grad_hidden_norm, grad_gain_two = norm_backward(hidden, factor_two, gains[1], grad_normed_two)
    grad_hidden = grad_rows + grad_hidden_norm
    grad_attn = grad_hidden.astype(low)
    terms = jnp.einsum(
        "stf,ghf->sgth",
        grad_attn.reshape(seqs_row, LEN, width),
        out_row,
        preferred_element_type=jnp.float32,
    )
    terms = terms.astype(low).reshape(col_n * LEN, -1)
    grad_heads = lax.psum_scatter(terms, "col", scatter_dimension=0, tiled=True)
    full_top = jnp.full((KVH, GROUP), -1e30, jnp.float32)
    full_top = lax.dynamic_update_slice(
        full_top, jnp.max(tops, axis=(1, 2))[None], (group_i, jnp.zeros((), jnp.int32))
    )
    far_out_sums, slot_out = token_sums(1, after(slot_out, terms), 1)
    far_out_sums = far_out_sums.astype(low)
    far_out_sums = jnp.broadcast_to(far_out_sums, (dh_n,) + far_out_sums.shape)
    grad_heads = after(grad_heads, far_out_sums)
    far_out_sums = to_owners(far_out_sums, "dh")
    grad_packed = attend_backward(packed, ids, log_total, grad_heads)
    packed_all = lax.all_gather(grad_packed, "col", axis=0).reshape(seqs_row, KVH, LEN, -1)

    own_out_sums, _ = token_sums(0, after(slot_out, grad_packed))
    packed_all = after(packed_all, own_out_sums)
    grad_down = block_grads(after(down_grad, far_out_sums))

    def owner_sums(left, right):
        columns = right.shape[-1]

        def term(k):
            group = lax.dynamic_index_in_dim(right, (row_i + k) % row_n, 1, False)
            return jnp.einsum("stf,sth->fh", left, group, preferred_element_type=jnp.float32)

        total = None
        for k in range(1, row_n):
            part = term(k)
            left = after(left, part)
            part = lax.ppermute(part, "row", [(i, (i + k) % row_n) for i in range(row_n)])
            total = part if total is None else total + part
        return (term(0) + total).astype(low)

    def dp_sums(total):
        parts = to_owners(total, ("dh", "dl")).reshape(dp_n, -1, total.shape[1])
        return jnp.sum(parts.astype(jnp.float32), axis=0)

    grad_normed_one = jnp.einsum(
        "sgth,gfh->stf", packed_all, qkv_row, preferred_element_type=jnp.float32
    ).reshape(tokens_row, width)
    out_total = owner_sums(grad_attn.reshape(seqs_row, LEN, width), after(heads, grad_heads))
    grad_gate_up = jnp.swapaxes(block_grads(after(in_grad, packed_all)), 1, 2)
    grad_gate_up = with_layout_constraint(grad_gate_up, Layout((0, 1, 2, 3)))
    qkv_total = owner_sums(normed_one.reshape(seqs_row, LEN, width), packed_all)
    far_out_sums = after(far_out_sums, qkv_total)
    far_out_sums = lax.dynamic_index_in_dim(far_out_sums, dh_n - 1 - dh_i, 0, False)
    block_output = hidden + own_out_sums + far_out_sums.astype(jnp.float32)
    totals = after(jnp.concatenate([qkv_total, out_total], axis=1), grad_gate_up)
    grad_gate_up, grad_down = after(grad_gate_up, qkv_total), after(grad_down, qkv_total)
    totals = dp_sums(totals)
    grad_qkv, grad_out = totals[:, None, : qkv_total.shape[1]], totals[:, qkv_total.shape[1] :].T[None]
    grad_normed_one = after(grad_normed_one, qkv_total)
    grad_input_norm, grad_gain_one = norm_backward(inputs, factor_one, gains[0], grad_normed_one)
    input_grad = grad_hidden + grad_input_norm

    tops_row = jnp.pad(full_top.reshape(1, -1), ((0, 0), (0, width - KVH * GROUP)))
    small = jnp.concatenate([grad_gain_one[None], grad_gain_two[None], tops_row])

    def combine(left, right):
        return jnp.concatenate([left[:2] + right[:2], jnp.maximum(left[2:], right[2:])])

    small = butterfly(small, combine, ("row", "dh", "dl"))
    grad_gains, head_top = small[:2], small[2, : KVH * GROUP].reshape(KVH, GROUP)
    head_top = butterfly(head_top, jnp.maximum, ("col",))

    factors = TAU_CLIP / jnp.maximum(head_top, TAU_CLIP)
    local_factors = lax.dynamic_slice_in_dim(factors, row_i, 1, 0)
    query_scale = jnp.repeat(jnp.sqrt(local_factors), HD, axis=1)
    key_scale = jnp.repeat(jnp.sqrt(jnp.min(local_factors, axis=1, keepdims=True)), HD, axis=1)
    column_scale = jnp.concatenate([query_scale, key_scale, jnp.ones_like(key_scale)], axis=1)
    qkv_new, qkv_one, qkv_two = adam_step(
        qkv_master, qkv_first, qkv_second, grad_qkv, D ** (-0.5), DECAY_RATE
    )
    qkv_new = qkv_new * column_scale[None]
    out_new, out_one, out_two = adam_step(
        out_master, out_first, out_second, grad_out, max(D // 192, 1) ** (-0.5), DECAY_RATE
    )
    gate_up_new, gate_up_one, gate_up_two = adam_step(
        gate_up_master, gate_up_first, gate_up_second, grad_gate_up, D ** (-0.5), DECAY_RATE
    )
    down_new, down_one, down_two = adam_step(
        down_master, down_first, down_second, grad_down, FFE ** (-0.5), DECAY_RATE
    )
    gains_new, gains_one, gains_two = adam_step(
        gains, gain_first, gain_second, grad_gains, 0.2, 0.0
    )
    return (
        block_output.reshape(1, -1, 2 * width),
        input_grad.reshape(1, -1, 2 * width),
        qkv_new,
        qkv_one,
        qkv_two,
        qkv_new.astype(jnp.bfloat16),
        out_new,
        out_one,
        out_two,
        out_new.astype(jnp.bfloat16),
        gate_up_new,
        gate_up_one,
        gate_up_two,
        gate_up_new.astype(jnp.bfloat16),
        down_new,
        down_one,
        down_two,
        down_new.astype(jnp.bfloat16),
        gains_new,
        gains_one,
        gains_two,
        factors.reshape(-1),
    )


def solution(mesh):
    devices = mesh.devices
    devices = devices.reshape((2, devices.shape[0] // 2) + devices.shape[1:])
    mesh = jax.sharding.Mesh(devices, ("dh", "dl", "row", "col"))
    dp = ("dh", "dl")
    in_specs = (
        P("col", (*dp, "row"), None),
        P("col", (*dp, "row"), None),
        P(None, dp),
        P(None, dp),
        P((*dp, "col"), None),
        P("col", "row", None),
        P("row", None, "col"),
        P(None, "col", None, "row"),
        P(None, "row", "col"),
        P(None, "col"),
        P(None, "col"),
        P(None, "col"),
        P(("col", *dp), "row", None),
        P(("col", *dp), "row", None),
        P(("col", *dp), "row", None),
        P("row", None, ("col", *dp)),
        P("row", None, ("col", *dp)),
        P("row", None, ("col", *dp)),
        P(dp, "col", None, "row"),
        P(dp, "col", None, "row"),
        P(dp, "col", None, "row"),
        P(dp, "row", "col"),
        P(dp, "row", "col"),
        P(dp, "row", "col"),
    )
    out_specs = (
        P("col", (*dp, "row"), None),
        P("col", (*dp, "row"), None),
        P(("col", *dp), "row", None),
        P(("col", *dp), "row", None),
        P(("col", *dp), "row", None),
        P(("col", *dp), "row", None),
        P("row", None, ("col", *dp)),
        P("row", None, ("col", *dp)),
        P("row", None, ("col", *dp)),
        P("row", None, ("col", *dp)),
        P(dp, "col", None, "row"),
        P(dp, "col", None, "row"),
        P(dp, "col", None, "row"),
        P(dp, "col", None, "row"),
        P(dp, "row", "col"),
        P(dp, "row", "col"),
        P(dp, "row", "col"),
        P(dp, "row", "col"),
        P(None, "col"),
        P(None, "col"),
        P(None, "col"),
        P(),
    )
    return jax.shard_map(
        on_device, mesh=mesh, in_specs=in_specs, out_specs=out_specs, check_vma=False
    )
```
